32 devices in a mesh: fsdp: 4 (over y, x), tensor: 8 (over z, core).
Axes of the slice: x: 2, y: 2, z: 4, core: 2. Of those that a mesh axis runs over, the one named last changes fastest.
Arguments:
- tokens: bfloat16 [768, 8192], P(('fsdp', 'tensor')), may hold values from -6 to 6
- out_grad: bfloat16 [768, 8192], P(('fsdp', 'tensor')), may hold values from -6 to 6
- up_weight: bfloat16 [256, 8, 128, 128], P('tensor', 'fsdp'), may hold values from -0.1875 to 0.1875
- down_weight: bfloat16 [256, 8, 128, 128], P('tensor', 'fsdp'), may hold values from -0.09375 to 0.09375
- up_index: int32 [256, 8], P('tensor'), may hold values from 0 to 63, all different within a row
- down_index: int32 [256, 8], P('tensor'), may hold values from 0 to 63, all different within a row
Outputs:
- mixed: bfloat16 [768, 8192], P(('fsdp', 'tensor'))
- input_grad: bfloat16 [768, 8192], P(('fsdp', 'tensor'))
- up_grad: float32 [256, 8, 128, 128], P('tensor', 'fsdp')
- down_grad: float32 [256, 8, 128, 128], P('tensor', 'fsdp')
The draws below stay inside these ranges and needn't reach their ends.
Inputs may be any that keep to these rules, and one draw needn't show every extreme that they name: Each row of up_index names 8 different input blocks; every block is named somewhere. Each row of down_index names 8 different output blocks; every block is named somewhere.
All inputs are finite; a program needn't handle non-finite values.
Results may differ from the reference program's by a relative error of at most 0.024.
Values may be sent and summed in bfloat16 or wider, within the bound.
No kernel may reach another device: no remote copies, remote signals or barrier semaphores. Data moves between devices by JAX's collectives and lax.ppermute only.
A program may use at most 192 MiB of HBM per device.

```python
import jax
import jax.numpy as jnp
from jax import lax

D = 8192
BLK = 128
K = 8
DB = 64
HB = 256
ROWS = 192
TOKENS = 768
N_FSDP = 4
N_TENSOR = 8


def level_of(key, dims, shards, least, high):
    factor_of = 1.0
    for position, parts in shards:
        steps = jax.random.uniform(jax.random.fold_in(jax.random.fold_in(key, 6), position), (parts,), jnp.float32, least / len(shards), high / len(shards))
        factor_of = factor_of * jnp.repeat(jnp.exp(steps), dims[position] // parts).reshape((-1,) + (1,) * (len(dims) - 1 - position))
    return factor_of


def different_ones(stream_key, rows, count, top, lift):
    order = jax.random.permutation(jax.random.fold_in(stream_key, 1), count)
    favour = order
    for power in range(3):
        favour = favour * favour // count
    favour = favour * lift // count
    chance = jax.random.randint(jax.random.fold_in(stream_key, 2), (rows, count), 0, 4096) + favour
    sure = jax.random.permutation(jax.random.fold_in(stream_key, 3), rows)[jnp.arange(count) % rows]
    chance = jnp.where(jnp.arange(rows)[:, None] == sure[None, :], 1 << 14, chance)
    priority = chance * count + jnp.arange(count)
    return lax.top_k(priority.astype(jnp.int32), top)[1].astype(jnp.int32)


def normal_values(stream_key, extent, scale, limit, shards=(), kind=jnp.bfloat16):
    values = scale * jax.random.normal(stream_key, extent, jnp.float32)
    if shards:
        values = values * level_of(stream_key, extent, shards, -0.22, 0.18)
    return jnp.clip(values, -limit, limit).astype(kind)


def setup_inputs(seed: int = 0) -> dict:
    arg_keys = jax.random.split(jax.random.key(seed), 7)
    return {
        "tokens": normal_values(arg_keys[0], (TOKENS, D), 1.0, 6.0, ((0, 32),)),
        "out_grad": normal_values(arg_keys[1], (TOKENS, D), 1.0, 6.0, ((0, 32),)),
        "up_weight": normal_values(arg_keys[2], (HB, K, BLK, BLK), (K * BLK) ** -0.5, 0.1875, ((0, 8), (1, 4))),
        "down_weight": normal_values(arg_keys[3], (HB, K, BLK, BLK), (HB * K * BLK // DB) ** -0.5, 0.09375, ((0, 8), (1, 4))),
        "up_index": different_ones(arg_keys[4], HB, DB, K, 0),
        "down_index": different_ones(arg_keys[5], HB, DB, K, 0),
    }


def reference(tokens, out_grad, up_weight, down_weight, up_index, down_index):
    input_blocks = tokens.reshape(TOKENS, DB, BLK)
    grad_blocks = out_grad.reshape(TOKENS, DB, BLK)
    per_group = HB // N_TENSOR

    def group_round(slot_terms):
        rounded = lax.optimization_barrier(slot_terms.astype(jnp.bfloat16))
        return jnp.sum(rounded.astype(jnp.float32), axis=0)

    def block_step(carried, scan_items):
        mixed_part, input_part = carried
        up_tile, down_tile, up_row, down_row = scan_items
        chosen = jnp.take(input_blocks, up_row, axis=1)
        preact = jnp.einsum('tki,kio->to', chosen.astype(jnp.float32), up_tile.astype(jnp.float32))
        hidden = jax.nn.silu(preact).astype(jnp.bfloat16)
        outward = jnp.einsum('to,koj->tkj', hidden.astype(jnp.float32), down_tile.astype(jnp.float32))
        mixed_part = mixed_part.at[:, down_row].add(outward)
        picked = jnp.take(grad_blocks, down_row, axis=1)
        hidden_grad = jnp.einsum('tkj,koj->to', picked.astype(jnp.float32), down_tile.astype(jnp.float32))
        gate_sigma = jax.nn.sigmoid(preact)
        pre_grad = (hidden_grad * gate_sigma * (1.0 + preact * (1.0 - gate_sigma))).astype(jnp.bfloat16)
        backward = jnp.einsum('to,kio->tki', pre_grad.astype(jnp.float32), up_tile.astype(jnp.float32))
        input_part = input_part.at[:, up_row].add(backward)
        chosen_g = chosen.astype(jnp.float32).reshape(N_FSDP, ROWS, K, BLK)
        pre_g = pre_grad.astype(jnp.float32).reshape(N_FSDP, ROWS, BLK)
        hidden_g = hidden.astype(jnp.float32).reshape(N_FSDP, ROWS, BLK)
        picked_g = picked.astype(jnp.float32).reshape(N_FSDP, ROWS, K, BLK)
        up_terms = group_round(jnp.einsum('grki,gro->gkio', chosen_g, pre_g))
        down_terms = group_round(jnp.einsum('gro,grkj->gkoj', hidden_g, picked_g))
        return (mixed_part, input_part), (up_terms, down_terms)

    def group_step(totals, group_items):
        empty = (jnp.zeros((TOKENS, DB, BLK), jnp.float32), jnp.zeros((TOKENS, DB, BLK), jnp.float32))
        (mixed_part, input_part), grads = lax.scan(block_step, empty, group_items)
        mixed_total = totals[0] + lax.optimization_barrier(mixed_part.astype(jnp.bfloat16)).astype(jnp.float32)
        input_total = totals[1] + lax.optimization_barrier(input_part.astype(jnp.bfloat16)).astype(jnp.float32)
        return (mixed_total, input_total), grads

    group_items = (up_weight.reshape(N_TENSOR, per_group, K, BLK, BLK),
                   down_weight.reshape(N_TENSOR, per_group, K, BLK, BLK),
                   up_index.reshape(N_TENSOR, per_group, K),
                   down_index.reshape(N_TENSOR, per_group, K))
    begin = (jnp.zeros((TOKENS, DB, BLK), jnp.float32), jnp.zeros((TOKENS, DB, BLK), jnp.float32))
    (mixed_total, input_total), (up_grad, down_grad) = lax.scan(group_step, begin, group_items)
    mixed = mixed_total.reshape(TOKENS, D).astype(jnp.bfloat16)
    input_grad = input_total.reshape(TOKENS, D).astype(jnp.bfloat16)
    return mixed, input_grad, up_grad.reshape(HB, K, BLK, BLK), down_grad.reshape(HB, K, BLK, BLK)
```

```python
import functools

import jax
import jax.numpy as jnp
from jax import lax
from jax.experimental import pallas as pl
from jax.experimental.pallas import tpu as pltpu
from jax.sharding import PartitionSpec as P

BLK = 128
CHUNKS = 4
MIB = 1 << 20
NT = (((1,), (1,)), ((), ()))
TN = (((0,), (0,)), ((), ()))


def dot(a, b, dims=(((1,), (0,)), ((), ()))):
    return lax.dot_general(a, b, dims, preferred_element_type=jnp.float32)


def columns(ref, blocks, offset=0):
    parts = [ref[:, pl.ds(pl.multiple_of(b * BLK + offset, BLK), BLK)] for b in blocks]
    return parts[0] if len(parts) == 1 else jnp.concatenate(parts, axis=1)


def side_by_side(ref, j, slots):
    parts = [ref[j, s] for s in range(slots)]
    return parts[0] if len(parts) == 1 else jnp.concatenate(parts, axis=1)


def forward_kernel(n, first, per_step, me_ref, up_idx, down_idx, rows_ref, *refs):
    ups, downs, out_ref = refs[:n], refs[n : 2 * n], refs[2 * n]
    slots = ups[0].shape[1]
    width = rows_ref.shape[1] // 2
    me = me_ref[0]
    for jj in range(per_step):
        j = first + pl.program_id(0) * per_step + jj
        pre = jnp.zeros((rows_ref.shape[0], BLK), jnp.float32)
        grad = jnp.zeros((rows_ref.shape[0], BLK), jnp.float32)
        for r in range(n):
            k = (me ^ r) * slots
            chosen = columns(rows_ref, [up_idx[j, k + s] for s in range(slots)])
            pre = pre + dot(chosen, ups[r][jj].reshape(slots * BLK, BLK))
            picked = columns(rows_ref, [down_idx[j, k + s] for s in range(slots)], width)
            grad = grad + dot(picked, side_by_side(downs[r], jj, slots), NT)
        sigma = jax.nn.sigmoid(pre)
        out_ref[0, jj] = (pre * sigma).astype(jnp.bfloat16)
        out_ref[1, jj] = (grad * sigma * (1.0 + pre * (1.0 - sigma))).astype(jnp.bfloat16)


def grad_kernel(n, first, per_step, me_ref, up_idx, down_idx, mine, other, h_mine, h_other, *outs):
    slots = outs[0].shape[1]
    width = mine.shape[1] // 2
    me = me_ref[0]
    for jj in range(per_step):
        j = first + pl.program_id(0) * per_step + jj
        for e, r in enumerate(range(0, n, 2)):
            k = (me ^ r) * slots
            up_cols = [up_idx[j, k + s] for s in range(slots)]
            down_cols = [down_idx[j, k + s] for s in range(slots)]
            up = dot(columns(mine, up_cols), h_mine[1, jj], TN)
            up = up + dot(columns(other, up_cols), h_other[1, jj], TN)
            down = dot(h_mine[0, jj], columns(mine, down_cols, width), TN)
            down = down + dot(h_other[0, jj], columns(other, down_cols, width), TN)
            for s in range(slots):
                up_tile = up[s * BLK : (s + 1) * BLK]
                down_tile = down[:, s * BLK : (s + 1) * BLK]
                if e == 0:
                    outs[0][jj, s] = up_tile
                    outs[1][jj, s] = down_tile
                else:
                    outs[1 + e][0, jj, s] = up_tile.astype(jnp.bfloat16)
                    outs[1 + e][1, jj, s] = down_tile.astype(jnp.bfloat16)


def spread_kernel(n, chunks, per_chunk, which, me_ref, idx, *refs):
    hs, ws = refs[:chunks], refs[chunks : chunks + chunks * n]
    out_ref, acc = refs[-2], refs[-1]
    slots = ws[0].shape[1]
    me = me_ref[0]
    step = pl.program_id(0)

    @pl.when(step == 0)
    def _():
        acc[...] = jnp.zeros_like(acc)

    for c in range(chunks):
        j = c * per_chunk + step
        h = hs[c][0, 0]
        for r in range(n):
            k = (me ^ r) * slots
            w = ws[c * n + r]
            if which == 0:
                terms = dot(h, side_by_side(w, 0, slots))
            else:
                terms = dot(h, w[0].reshape(slots * BLK, BLK), NT)
            for s in range(slots):
                at = pl.ds(pl.multiple_of(idx[j, k + s] * BLK, BLK), BLK)
                acc[:, at] += terms[:, s * BLK : (s + 1) * BLK]

    @pl.when(step == pl.num_programs(0) - 1)
    def _():
        out_ref[...] = acc[...].astype(out_ref.dtype)


def smem():
    return pl.BlockSpec(memory_space=pltpu.SMEM)


def whole(shape):
    return pl.BlockSpec(shape, lambda i: (0,) * len(shape), pipeline_mode=pl.Buffered(1))


def params():
    return pltpu.CompilerParams(vmem_limit_bytes=48 * MIB)


def forward(n, first, me, up_index, down_index, rows, ups, downs):
    per_chunk, slots = ups[0].shape[:2]
    count = rows.shape[0]
    per_step = 2
    tile = pl.BlockSpec((per_step, slots, BLK, BLK), lambda i: (i, 0, 0, 0))
    flops = 4 * count * per_chunk * slots * n * BLK * BLK
    return pl.pallas_call(
        functools.partial(forward_kernel, n, first, per_step),
        grid=(per_chunk // per_step,),
        in_specs=[smem()] * 3 + [whole(rows.shape)] + [tile] * (2 * n),
        out_specs=pl.BlockSpec((2, per_step, count, BLK), lambda i: (0, i, 0, 0)),
        out_shape=jax.ShapeDtypeStruct((2, per_chunk, count, BLK), jnp.bfloat16),
        compiler_params=params(),
        cost_estimate=pl.CostEstimate(flops=flops, bytes_accessed=10 * MIB, transcendentals=0),
        name="forward_chunk",
    )(me, up_index, down_index, rows, *ups, *downs)


def grads(n, first, me, up_index, down_index, mine, other, h_mine, h_other, slots):
    per_chunk, count = h_mine.shape[1:3]
    per_step = 2
    h_spec = pl.BlockSpec((2, per_step, count, BLK), lambda i: (0, i, 0, 0))
    own = pl.BlockSpec((per_step, slots, BLK, BLK), lambda i: (i, 0, 0, 0))
    sent = pl.BlockSpec((2, per_step, slots, BLK, BLK), lambda i: (0, i, 0, 0, 0))
    own_shape = jax.ShapeDtypeStruct((per_chunk, slots, BLK, BLK), jnp.float32)
    sent_shape = jax.ShapeDtypeStruct((2, per_chunk, slots, BLK, BLK), jnp.bfloat16)
    flops = 4 * count * per_chunk * slots * n * BLK * BLK
    return pl.pallas_call(
        functools.partial(grad_kernel, n, first, per_step),
        grid=(per_chunk // per_step,),
        in_specs=[smem()] * 3 + [whole(mine.shape)] * 2 + [h_spec] * 2,
        out_specs=[own] * 2 + [sent] * (n // 2 - 1),
        out_shape=[own_shape] * 2 + [sent_shape] * (n // 2 - 1),
        compiler_params=params(),
        cost_estimate=pl.CostEstimate(flops=flops, bytes_accessed=18 * MIB, transcendentals=0),
        name="grad_chunk",
    )(me, up_index, down_index, mine, other, h_mine, h_other)


def spread(n, which, me, index, hs, ws, width):
    chunks = len(hs)
    per_chunk, count = hs[0].shape[1:3]
    slots = ws[0][0].shape[1]
    tile = pl.BlockSpec((1, slots, BLK, BLK), lambda i: (i, 0, 0, 0))
    h_spec = pl.BlockSpec((1, 1, count, BLK), lambda i: (which, i, 0, 0))
    flops = 2 * count * per_chunk * chunks * slots * n * BLK * BLK
    return pl.pallas_call(
        functools.partial(spread_kernel, n, chunks, per_chunk, which),
        grid=(per_chunk,),
        in_specs=[smem()] * 2 + [h_spec] * chunks + [tile] * (chunks * n),
        out_specs=whole((count, width)),
        out_shape=jax.ShapeDtypeStruct((count, width), jnp.bfloat16),
        scratch_shapes=[pltpu.VMEM((count, width), jnp.float32)],
        compiler_params=params(),
        cost_estimate=pl.CostEstimate(flops=flops, bytes_accessed=14 * MIB, transcendentals=0),
        name="spread",
    )(me, index, *hs, *[w for chunk in ws for w in chunk])


def exchange(a, bit, n):
    return lax.ppermute(a, "fsdp", [(i, i ^ bit) for i in range(n)])


def gather(a, n, bits):
    held = {0: a}
    for bit in bits:
        for r in list(held):
            held[r ^ bit] = exchange(held[r], bit, n)
    return [held[r] for r in range(n)]


def body(n, tokens, out_grad, up_weight, down_weight, up_index, down_index):
    width = tokens.shape[1]
    slots = up_weight.shape[1]
    chunks = CHUNKS
    per_chunk = up_weight.shape[0] // chunks
    bits = [1 << b for b in range(n.bit_length() - 1)]
    me = lax.axis_index("fsdp").astype(jnp.int32).reshape(1)

    both = jnp.concatenate([tokens, out_grad], axis=1)
    mine = lax.all_gather(both, "tensor", axis=0, tiled=True)
    other = lax.all_gather(exchange(both, 1, n), "tensor", axis=0, tiled=True)

    ups, downs, hs, ups_grad, downs_grad = [], [], [], [], []
    for c in range(chunks):
        part = slice(c * per_chunk, (c + 1) * per_chunk)
        ups.append(gather(up_weight[part], n, bits))
        downs.append(gather(down_weight[part], n, bits[::-1]))
        hs.append(forward(n, c * per_chunk, me, up_index, down_index, mine, ups[c], downs[c]))

    mixed = spread(n, 0, me, down_index, hs, downs, width)
    mixed_rows = lax.psum_scatter(mixed, "tensor", scatter_dimension=0, tiled=True)
    spread_in = spread(n, 1, me, up_index, hs, ups, width)
    input_rows = lax.psum_scatter(spread_in, "tensor", scatter_dimension=0, tiled=True)

    for c in range(chunks):
        h_other = exchange(hs[c], 1, n)
        up, down, *sent = grads(
            n, c * per_chunk, me, up_index, down_index, mine, other, hs[c], h_other, slots
        )
        for e, part in enumerate(sent):
            got = exchange(part, 2 * (e + 1), n).astype(jnp.float32)
            up, down = up + got[0], down + got[1]
        ups_grad.append(up)
        downs_grad.append(down)
    up_grad = jnp.concatenate(ups_grad, axis=0)
    down_grad = jnp.concatenate(downs_grad, axis=0)
    return (mixed_rows, input_rows, up_grad, down_grad)


def solution(mesh):
    return jax.shard_map(
        functools.partial(body, mesh.shape["fsdp"]),
        mesh=mesh,
        in_specs=(
            P(("fsdp", "tensor"), None),
            P(("fsdp", "tensor"), None),
            P("tensor", "fsdp", None, None),
            P("tensor", "fsdp", None, None),
            P("tensor", None),
            P("tensor", None),
        ),
        out_specs=(
            P(("fsdp", "tensor"), None),
            P(("fsdp", "tensor"), None),
            P("tensor", "fsdp", None, None),
            P("tensor", "fsdp", None, None),
        ),
        check_vma=False,
    )
```

```python
import functools

import jax
import jax.numpy as jnp
from jax import lax
from jax.experimental import pallas as pl
from jax.experimental.pallas import tpu as pltpu
from jax.sharding import PartitionSpec as P

BLK = 128
CHUNKS = 4
MIB = 1 << 20
NT = (((1,), (1,)), ((), ()))
TN = (((0,), (0,)), ((), ()))


def dot(a, b, dims=(((1,), (0,)), ((), ()))):
    return lax.dot_general(a, b, dims, preferred_element_type=jnp.float32)


def columns(ref, blocks, offset=0):
    parts = [ref[:, pl.ds(pl.multiple_of(b * BLK + offset, BLK), BLK)] for b in blocks]
    return parts[0] if len(parts) == 1 else jnp.concatenate(parts, axis=1)


def side_by_side(ref, j, slots):
    parts = [ref[j, s] for s in range(slots)]
    return parts[0] if len(parts) == 1 else jnp.concatenate(parts, axis=1)


def hidden_pair(n, j, jj, me, up_idx, down_idx, rows, ups, downs):
    slots = ups[0].shape[1]
    width = rows.shape[1] // 2
    pre = jnp.zeros((rows.shape[0], BLK), jnp.float32)
    grad = jnp.zeros((rows.shape[0], BLK), jnp.float32)
    for r in range(n):
        k = (me ^ r) * slots
        chosen = columns(rows, [up_idx[j, k + s] for s in range(slots)])
        pre = pre + dot(chosen, ups[r][jj].reshape(slots * BLK, BLK))
        picked = columns(rows, [down_idx[j, k + s] for s in range(slots)], width)
        grad = grad + dot(picked, side_by_side(downs[r], jj, slots), NT)
    sigma = jax.nn.sigmoid(pre)
    hidden = (pre * sigma).astype(jnp.bfloat16)
    return hidden, (grad * sigma * (1.0 + pre * (1.0 - sigma))).astype(jnp.bfloat16)


def forward_kernel(n, first, per_step, me_ref, up_idx, down_idx, rows, *refs):
    ups, downs, out_ref = refs[:n], refs[n : 2 * n], refs[2 * n]
    for jj in range(per_step):
        j = first + pl.program_id(0) * per_step + jj
        hidden, pre_grad = hidden_pair(n, j, jj, me_ref[0], up_idx, down_idx, rows, ups, downs)
        out_ref[0, jj] = hidden
        out_ref[1, jj] = pre_grad


def grad_kernel(n, first, per_step, me_ref, up_idx, down_idx, mine, other, h_mine, *refs):
    ups, downs, outs = refs[:n], refs[n : 2 * n], refs[2 * n :]
    slots = outs[0].shape[1]
    width = mine.shape[1] // 2
    me = me_ref[0]
    for jj in range(per_step):
        j = first + pl.program_id(0) * per_step + jj
        hidden, pre_grad = hidden_pair(n, j, jj, me, up_idx, down_idx, other, ups, downs)
        for e, r in enumerate(range(0, n, 2)):
            k = (me ^ r) * slots
            up_cols = [up_idx[j, k + s] for s in range(slots)]
            down_cols = [down_idx[j, k + s] for s in range(slots)]
            up = dot(columns(mine, up_cols), h_mine[1, jj], TN)
            up = up + dot(columns(other, up_cols), pre_grad, TN)
            down = dot(h_mine[0, jj], columns(mine, down_cols, width), TN)
            down = down + dot(hidden, columns(other, down_cols, width), TN)
            for s in range(slots):
                up_tile = up[s * BLK : (s + 1) * BLK]
                down_tile = down[:, s * BLK : (s + 1) * BLK]
                if e == 0:
                    outs[0][jj, s] = up_tile
                    outs[1][jj, s] = down_tile
                else:
                    outs[1 + e][0, jj, s] = up_tile.astype(jnp.bfloat16)
                    outs[1 + e][1, jj, s] = down_tile.astype(jnp.bfloat16)


def spread_kernel(n, firsts, which, per_step, me_ref, idx, *refs):
    chunks = len(firsts)
    hs, ws = refs[:chunks], refs[chunks : chunks + chunks * n]
    out_ref, acc = refs[-2:]
    slots = ws[0].shape[1]
    me = me_ref[0]
    step = pl.program_id(0)

    @pl.when(step == 0)
    def _():
        @pl.loop(0, acc.shape[0] // 16)
        def _(i):
            acc[pl.ds(pl.multiple_of(i * 16, 16), 16)] = jnp.zeros((16, acc.shape[1]), acc.dtype)

    for c, first in enumerate(firsts):
        for jj in range(per_step):
            j = first + step * per_step + jj
            h = hs[c][0, jj]
            for r in range(n):
                k = (me ^ r) * slots
                w = ws[c * n + r]
                if which == 0:
                    terms = dot(h, side_by_side(w, jj, slots))
                else:
                    terms = dot(h, w[jj].reshape(slots * BLK, BLK), NT)
                for s in range(slots):
                    at = pl.ds(pl.multiple_of(idx[j, k + s] * BLK, BLK), BLK)
                    acc[:, at] += terms[:, s * BLK : (s + 1) * BLK]

    @pl.when(step == pl.num_programs(0) - 1)
    def _():
        @pl.loop(0, acc.shape[0] // 16)
        def _(i):
            at = pl.ds(pl.multiple_of(i * 16, 16), 16)
            out_ref[at] = acc[at].astype(out_ref.dtype)


def finish_kernel(count, own_up, own_down, *refs):
    up_ref, down_ref = refs[-2:]
    up, down = own_up[...], own_down[...]
    for got in refs[:count]:
        up = up + got[0].astype(jnp.float32)
        down = down + got[1].astype(jnp.float32)
    up_ref[...] = up
    down_ref[...] = down


def smem():
    return pl.BlockSpec(memory_space=pltpu.SMEM)


def whole(shape):
    return pl.BlockSpec(shape, lambda i: (0,) * len(shape), pipeline_mode=pl.Buffered(1))


def params():
    return pltpu.CompilerParams(vmem_limit_bytes=60 * MIB)


def forward(n, first, me, up_index, down_index, rows, ups, downs):
    per_chunk, slots = ups[0].shape[:2]
    count = rows.shape[0]
    per_step = 2
    tile = pl.BlockSpec((per_step, slots, BLK, BLK), lambda i: (i, 0, 0, 0))
    return pl.pallas_call(
        functools.partial(forward_kernel, n, first, per_step),
        grid=(per_chunk // per_step,),
        in_specs=[smem()] * 3 + [whole(rows.shape)] + [tile] * (2 * n),
        out_specs=pl.BlockSpec((2, per_step, count, BLK), lambda i: (0, i, 0, 0)),
        out_shape=jax.ShapeDtypeStruct((2, per_chunk, count, BLK), jnp.bfloat16),
        compiler_params=params(),
        cost_estimate=pl.CostEstimate(flops=0, bytes_accessed=MIB // 64, transcendentals=0),
        name="forward_chunk",
    )(me, up_index, down_index, rows, *ups, *downs)


def grads(n, first, me, up_index, down_index, mine, other, h_mine, ups, downs):
    per_chunk, slots = ups[0].shape[:2]
    count = h_mine.shape[2]
    per_step = 2
    h_spec = pl.BlockSpec((2, per_step, count, BLK), lambda i: (0, i, 0, 0))
    tile = pl.BlockSpec((per_step, slots, BLK, BLK), lambda i: (i, 0, 0, 0))
    sent = pl.BlockSpec((2, per_step, slots, BLK, BLK), lambda i: (0, i, 0, 0, 0))
    own_shape = jax.ShapeDtypeStruct((per_chunk, slots, BLK, BLK), jnp.float32)
    sent_shape = jax.ShapeDtypeStruct((2, per_chunk, slots, BLK, BLK), jnp.bfloat16)
    return pl.pallas_call(
        functools.partial(grad_kernel, n, first, per_step),
        grid=(per_chunk // per_step,),
        in_specs=[smem()] * 3 + [whole(mine.shape)] * 2 + [h_spec] + [tile] * (2 * n),
        out_specs=[tile] * 2 + [sent] * (n // 2 - 1),
        out_shape=[own_shape] * 2 + [sent_shape] * (n // 2 - 1),
        compiler_params=params(),
        cost_estimate=pl.CostEstimate(flops=0, bytes_accessed=MIB // 64, transcendentals=0),
        name="grad_chunk",
    )(me, up_index, down_index, mine, other, h_mine, *ups, *downs)


def spread(n, which, firsts, me, index, hs, ws, width):
    chunks = len(hs)
    per_chunk, count = hs[0].shape[1:3]
    slots = ws[0][0].shape[1]
    per_step = 2
    tile = pl.BlockSpec((per_step, slots, BLK, BLK), lambda i: (i, 0, 0, 0))
    h_spec = pl.BlockSpec((1, per_step, count, BLK), lambda i: (which, i, 0, 0))
    return pl.pallas_call(
        functools.partial(spread_kernel, n, firsts, which, per_step),
        grid=(per_chunk // per_step,),
        in_specs=[smem()] * 2 + [h_spec] * chunks + [tile] * (chunks * n),
        out_specs=whole((count, width)),
        out_shape=jax.ShapeDtypeStruct((count, width), jnp.bfloat16),
        scratch_shapes=[pltpu.VMEM((count, width), jnp.float32)],
        compiler_params=params(),
        cost_estimate=pl.CostEstimate(flops=0, bytes_accessed=MIB // 64, transcendentals=0),
        name="spread",
    )(me, index, *hs, *[w for chunk in ws for w in chunk])


def finish(first, blocks, up, down, got, done):
    per_chunk, slots = up.shape[:2]
    per_step = 4
    at = first // per_step
    own = pl.BlockSpec((per_step, slots, BLK, BLK), lambda i: (i, 0, 0, 0))
    sent = pl.BlockSpec((2, per_step, slots, BLK, BLK), lambda i: (0, i, 0, 0, 0))
    part = pl.BlockSpec((per_step, slots, BLK, BLK), lambda i: (at + i, 0, 0, 0))
    kept = pl.BlockSpec(memory_space=pl.ANY)
    shape = jax.ShapeDtypeStruct((blocks, slots, BLK, BLK), jnp.float32)
    return pl.pallas_call(
        functools.partial(finish_kernel, len(got)),
        grid=(per_chunk // per_step,),
        in_specs=[own] * 2 + [sent] * len(got) + [kept] * len(done),
        out_specs=[part] * 2,
        out_shape=[shape] * 2,
        input_output_aliases={2 + len(got) + i: i for i in range(len(done))},
        compiler_params=params(),
        cost_estimate=pl.CostEstimate(flops=0, bytes_accessed=MIB // 64, transcendentals=0),
        name="finish_chunk",
    )(up, down, *got, *done)


def after(a, *earlier):
    return lax.optimization_barrier((a,) + earlier)[0]


def exchange(a, bit, n):
    return lax.ppermute(a, "fsdp", [(i, i ^ bit) for i in range(n)])


def gather(n, a, bits):
    held = {0: a}
    for bit in bits:
        for r in list(held):
            if r ^ bit not in held:
                held[r ^ bit] = exchange(held[r], bit, n)
    return [held[r] for r in range(n)]


def body(n, tokens, out_grad, up_weight, down_weight, up_index, down_index):
    width = tokens.shape[1]
    blocks = up_weight.shape[0]
    chunks = CHUNKS
    per_chunk = blocks // chunks
    firsts = [c * per_chunk for c in range(chunks)]
    bits = [1 << b for b in range(n.bit_length() - 1)]
    me = lax.axis_index("fsdp").astype(jnp.int32).reshape(1)

    both = jnp.concatenate([tokens, out_grad], axis=1)
    mine = lax.all_gather(both, "tensor", axis=0, tiled=True)
    swapped = exchange(both, 1, n)

    ups, downs, hs = [], [], []
    for c in range(chunks):
        part = slice(firsts[c], firsts[c] + per_chunk)
        ups.append(gather(n, up_weight[part], bits))
        downs.append(gather(n, down_weight[part], bits[::-1]))
        if c == 0:
            marks = [ups[0][bits[0]], ups[0][bits[-1]], downs[0][bits[0]], downs[0][bits[-1]]]
            other = lax.all_gather(after(swapped, *marks), "tensor", axis=0, tiled=True)
        hs.append(forward(n, firsts[c], me, up_index, down_index, mine, ups[c], downs[c]))

    mixed = spread(n, 0, firsts, me, down_index, hs, downs, width)
    mixed_rows = lax.psum_scatter(mixed, "tensor", scatter_dimension=0, tiled=True)

    grad_out = ()
    for c in range(chunks):
        rows = other
        if c == 0:
            rows = after(other, mixed)
        if c == 1:
            rows = after(other, spread_in)
        up, down, *sent = grads(
            n, firsts[c], me, up_index, down_index, mine, rows, hs[c], ups[c], downs[c]
        )
        if c == 0:
            h_last = after(hs[-1], sent[0])
            spread_in = spread(n, 1, firsts, me, up_index, hs[:-1] + [h_last], ups, width)
            input_rows = lax.psum_scatter(spread_in, "tensor", scatter_dimension=0, tiled=True)
        got = [exchange(part, 2 * (e + 1), n) for e, part in enumerate(sent)]
        grad_out = finish(firsts[c], blocks, up, down, got, grad_out)
    return (mixed_rows, input_rows, *grad_out)


def solution(mesh):
    return jax.shard_map(
        functools.partial(body, mesh.shape["fsdp"]),
        mesh=mesh,
        in_specs=(
            P(("fsdp", "tensor"), None),
            P(("fsdp", "tensor"), None),
            P("tensor", "fsdp", None, None),
            P("tensor", "fsdp", None, None),
            P("tensor", None),
            P("tensor", None),
        ),
        out_specs=(
            P(("fsdp", "tensor"), None),
            P(("fsdp", "tensor"), None),
            P("tensor", "fsdp", None, None),
            P("tensor", "fsdp", None, None),
        ),
        check_vma=False,
    )
```

```python
import functools

import jax
import jax.numpy as jnp
from jax import lax
from jax.experimental import pallas as pl
from jax.experimental.pallas import tpu as pltpu
from jax.sharding import PartitionSpec as P

BLK = 128
CHUNKS = 4
MIB = 1 << 20
US = 3.69e6
NT = (((1,), (1,)), ((), ()))
TN = (((0,), (0,)), ((), ()))


def dot(a, b, dims=(((1,), (0,)), ((), ()))):
    return lax.dot_general(a, b, dims, preferred_element_type=jnp.float32)


def columns(ref, blocks, offset=0):
    parts = [ref[:, pl.ds(pl.multiple_of(b * BLK + offset, BLK), BLK)] for b in blocks]
    return parts[0] if len(parts) == 1 else jnp.concatenate(parts, axis=1)


def side_by_side(ref, j, slots):
    parts = [ref[j, s] for s in range(slots)]
    return parts[0] if len(parts) == 1 else jnp.concatenate(parts, axis=1)


def hidden_pair(n, j, jj, me, up_idx, down_idx, rows, ups, downs):
    slots = ups[0].shape[1]
    width = rows.shape[1] // 2
    pre = jnp.zeros((rows.shape[0], BLK), jnp.float32)
    grad = jnp.zeros((rows.shape[0], BLK), jnp.float32)
    for r in range(n):
        k = (me ^ r) * slots
        chosen = columns(rows, [up_idx[j, k + s] for s in range(slots)])
        pre = pre + dot(chosen, ups[r][jj].reshape(slots * BLK, BLK))
        picked = columns(rows, [down_idx[j, k + s] for s in range(slots)], width)
        grad = grad + dot(picked, side_by_side(downs[r], jj, slots), NT)
    sigma = jax.nn.sigmoid(pre)
    hidden = (pre * sigma).astype(jnp.bfloat16)
    return hidden, (grad * sigma * (1.0 + pre * (1.0 - sigma))).astype(jnp.bfloat16)


def add_spread(n, j, jj, me, idx, h, ws, total, offset, which):
    slots = ws[0].shape[1]
    for r in range(n):
        k = (me ^ r) * slots
        if which == 0:
            terms = dot(h, side_by_side(ws[r], jj, slots))
        else:
            terms = dot(h, ws[r][jj].reshape(slots * BLK, BLK), NT)
        for s in range(slots):
            at = pl.ds(pl.multiple_of(idx[j, k + s] * BLK + offset, BLK), BLK)
            total[:, at] += terms[:, s * BLK : (s + 1) * BLK]


def forward_kernel(n, firsts, resumed, me_ref, up_idx, down_idx, rows, *refs):
    groups = len(firsts)
    if resumed:
        partial, refs = refs[0], refs[1:]
    ups = [refs[2 * n * g : 2 * n * g + n] for g in range(groups)]
    downs = [refs[2 * n * g + n : 2 * n * (g + 1)] for g in range(groups)]
    hs, out_ref = refs[2 * n * groups : (2 * n + 1) * groups], refs[(2 * n + 1) * groups]
    total = refs[-2] if resumed else out_ref
    per_step = ups[0][0].shape[0]
    width = rows.shape[1] // 2
    step = pl.program_id(0)
    me = me_ref[0]
    if resumed:
        copy = pltpu.make_async_copy(partial, total, refs[-1])

    @pl.when(step == 0)
    def _():
        if resumed:
            copy.start()
        else:

            @pl.loop(0, total.shape[0] // 16)
            def _(i):
                at = pl.ds(pl.multiple_of(i * 16, 16), 16)
                total[at] = jnp.zeros((16, total.shape[1]), total.dtype)

    blocks = [(g, jj) for g in range(groups) for jj in range(per_step)]
    for g, jj in blocks:
        j = firsts[g] + step * per_step + jj
        hidden, pre_grad = hidden_pair(n, j, jj, me, up_idx, down_idx, rows, ups[g], downs[g])
        hs[g][0, jj] = hidden
        hs[g][1, jj] = pre_grad

    if resumed:

        @pl.when(step == 0)
        def _():
            copy.wait()

    for g, jj in blocks:
        j = firsts[g] + step * per_step + jj
        add_spread(n, j, jj, me, down_idx, hs[g][0, jj], downs[g], total, 0, 0)
        add_spread(n, j, jj, me, up_idx, hs[g][1, jj], ups[g], total, width, 1)

    if resumed:

        @pl.when(step == pl.num_programs(0) - 1)
        def _():
            @pl.loop(0, total.shape[0] // 16)
            def _(i):
                at = pl.ds(pl.multiple_of(i * 16, 16), 16)
                out_ref[at] = total[at].astype(out_ref.dtype)


def grad_kernel(n, first, per_step, half, me_ref, up_idx, down_idx, mine_hbm, other_hbm, h_mine, *refs):
    ups, downs, outs = refs[:n], refs[n : 2 * n], refs[2 * n : -4]
    mine, other, h_other, sems = refs[-4:]
    slots = ups[0].shape[1]
    width = mine.shape[1] // 2
    me = me_ref[0]
    step = pl.program_id(0)
    copies = [
        pltpu.make_async_copy(src.at[:, pl.ds(p * width, width)], dst.at[:, pl.ds(p * width, width)], sems.at[i])
        for i, (src, dst, p) in enumerate(
            ((other_hbm, other, 0), (other_hbm, other, 1), (mine_hbm, mine, 0), (mine_hbm, mine, 1))
        )
    ]

    @pl.when(step == 0)
    def _():
        for copy in copies:
            copy.start()
        copies[0].wait()
        copies[1].wait()

    @pl.when(step == half)
    def _():
        copies[2].wait()
        copies[3].wait()

    @pl.when(step < half)
    def _():
        for jj in range(per_step):
            at = step * per_step + jj
            hidden, pre_grad = hidden_pair(
                n, first + at, jj, me, up_idx, down_idx, other, ups, downs
            )
            h_other[0, at] = hidden
            h_other[1, at] = pre_grad

    @pl.when(step >= half)
    def _():
        for jj in range(per_step):
            at = (step - half) * per_step + jj
            j = first + at
            for e, r in enumerate(range(0, n, 2)):
                k = (me ^ r) * slots
                up_cols = [up_idx[j, k + s] for s in range(slots)]
                down_cols = [down_idx[j, k + s] for s in range(slots)]
                up = dot(columns(mine, up_cols), h_mine[1, jj], TN)
                up = up + dot(columns(other, up_cols), h_other[1, at], TN)
                down = dot(h_mine[0, jj], columns(mine, down_cols, width), TN)
                down = down + dot(h_other[0, at], columns(other, down_cols, width), TN)
                for s in range(slots):
                    up_tile = up[s * BLK : (s + 1) * BLK]
                    down_tile = down[:, s * BLK : (s + 1) * BLK]
                    if e == 0:
                        outs[0][jj, s] = up_tile
                        outs[1][jj, s] = down_tile
                    else:
                        outs[1 + e][0, jj, s] = up_tile.astype(jnp.bfloat16)
                        outs[1 + e][1, jj, s] = down_tile.astype(jnp.bfloat16)


def finish_kernel(count, own_up, own_down, *refs):
    up_ref, down_ref = refs[-2:]
    up, down = own_up[...], own_down[...]
    for got in refs[:count]:
        up = up + got[0].astype(jnp.float32)
        down = down + got[1].astype(jnp.float32)
    up_ref[...] = up
    down_ref[...] = down


def smem():
    return pl.BlockSpec(memory_space=pltpu.SMEM)


def whole(shape):
    return pl.BlockSpec(shape, lambda i: (0,) * len(shape), pipeline_mode=pl.Buffered(1))


def params():
    return pltpu.CompilerParams(vmem_limit_bytes=60 * MIB)


def tiles(piece, per_step, index):
    array, lead = piece
    slots = array.shape[-3]
    if lead is None:
        return pl.BlockSpec((per_step, slots, BLK, BLK), lambda i: (index(i), 0, 0, 0))
    return pl.BlockSpec((None, per_step, slots, BLK, BLK), lambda i: (lead, index(i), 0, 0, 0))


def forward(n, first, per_group, me, up_index, down_index, rows, ups, downs, partial=None):
    resumed = partial is not None
    count = rows.shape[0]
    per_step = min(4, per_group)
    h_spec = pl.BlockSpec((2, per_step, count, BLK), lambda i: (0, i, 0, 0))
    h_shape = jax.ShapeDtypeStruct((2, per_group, count, BLK), jnp.bfloat16)
    total = jax.ShapeDtypeStruct(rows.shape, jnp.bfloat16 if resumed else jnp.float32)
    scratch = [pltpu.VMEM(rows.shape, jnp.float32), pltpu.SemaphoreType.DMA]
    pieces = ups + downs
    return pl.pallas_call(
        functools.partial(forward_kernel, n, [first], resumed),
        grid=(per_group // per_step,),
        in_specs=[smem()] * 3
        + [whole(rows.shape)]
        + [pl.BlockSpec(memory_space=pl.ANY)] * resumed
        + [tiles(piece, per_step, lambda i: i) for piece in pieces],
        out_specs=[h_spec, whole(rows.shape)],
        out_shape=[h_shape, total],
        scratch_shapes=scratch * resumed,
        compiler_params=params(),
        cost_estimate=pl.CostEstimate(flops=0, bytes_accessed=int(20 * US), transcendentals=0),
        name="forward_last" if resumed else "forward_first",
    )(
        me,
        up_index,
        down_index,
        rows,
        *([partial] if resumed else []),
        *[array for array, _ in pieces],
    )


def grads(n, start, at, per_chunk, me, up_index, down_index, mine, other, h_mine, ups, downs):
    slots = ups[0][0].shape[-3]
    count = h_mine.shape[2]
    per_step = min(4, per_chunk)
    skip = at // per_step
    half = per_chunk // per_step

    def early(i):
        return jnp.minimum(i, half - 1)

    def late(i):
        return jnp.maximum(i - half, 0)

    h_spec = pl.BlockSpec((2, per_step, count, BLK), lambda i: (0, skip + late(i), 0, 0))
    pieces = ups + downs
    w_specs = [tiles(piece, per_step, lambda i: skip + early(i)) for piece in pieces]
    own = pl.BlockSpec((per_step, slots, BLK, BLK), lambda i: (late(i), 0, 0, 0))
    sent = pl.BlockSpec((2, per_step, slots, BLK, BLK), lambda i: (0, late(i), 0, 0, 0))
    own_shape = jax.ShapeDtypeStruct((per_chunk, slots, BLK, BLK), jnp.float32)
    sent_shape = jax.ShapeDtypeStruct((2, per_chunk, slots, BLK, BLK), jnp.bfloat16)
    return pl.pallas_call(
        functools.partial(grad_kernel, n, start + at, per_step, half),
        grid=(2 * half,),
        in_specs=[smem()] * 3 + [pl.BlockSpec(memory_space=pl.ANY)] * 2 + [h_spec] + w_specs,
        out_specs=[own] * 2 + [sent] * (n // 2 - 1),
        out_shape=[own_shape] * 2 + [sent_shape] * (n // 2 - 1),
        scratch_shapes=[
            pltpu.VMEM(mine.shape, mine.dtype),
            pltpu.VMEM(mine.shape, mine.dtype),
            pltpu.VMEM((2, per_chunk, count, BLK), jnp.bfloat16),
            pltpu.SemaphoreType.DMA((4,)),
        ],
        compiler_params=params(),
        cost_estimate=pl.CostEstimate(flops=0, bytes_accessed=int(12 * US), transcendentals=0),
        name="grad_chunk",
    )(me, up_index, down_index, mine, other, h_mine, *[array for array, _ in pieces])


def finish(first, blocks, up, down, got, done):
    per_chunk, slots = up.shape[:2]
    per_step = 4
    at = first // per_step
    own = pl.BlockSpec((per_step, slots, BLK, BLK), lambda i: (i, 0, 0, 0))
    sent = pl.BlockSpec((2, per_step, slots, BLK, BLK), lambda i: (0, i, 0, 0, 0))
    part = pl.BlockSpec((per_step, slots, BLK, BLK), lambda i: (at + i, 0, 0, 0))
    kept = pl.BlockSpec(memory_space=pl.ANY)
    shape = jax.ShapeDtypeStruct((blocks, slots, BLK, BLK), jnp.float32)
    return pl.pallas_call(
        functools.partial(finish_kernel, len(got)),
        grid=(per_chunk // per_step,),
        in_specs=[own] * 2 + [sent] * len(got) + [kept] * len(done),
        out_specs=[part] * 2,
        out_shape=[shape] * 2,
        input_output_aliases={2 + len(got) + i: i for i in range(len(done))},
        compiler_params=params(),
        cost_estimate=pl.CostEstimate(flops=0, bytes_accessed=int(3 * US), transcendentals=0),
        name="finish_chunk",
    )(up, down, *got, *done)


def after(a, *earlier):
    return lax.optimization_barrier((a,) + earlier)[0]


def exchange(a, bit, n):
    return lax.ppermute(a, "fsdp", [(i, i ^ bit) for i in range(n)])


def gather(n, up, down, late=()):
    bits = [1 << b for b in range(n.bit_length() - 1)]
    first, last = bits[0], bits[-1]
    ups = {0: up, first: exchange(up, first, n), last: exchange(up, last, n)}
    downs = {0: down, first: exchange(down, first, n), last: exchange(down, last, n)}
    marks = [ups[first], downs[last], ups[last], downs[first]]
    for held, order in ((ups, bits[1:]), (downs, bits[-2::-1])):
        for bit in order:
            for r in list(held):
                if r ^ bit not in held:
                    a = after(held[r], *marks, *late) if late else held[r]
                    held[r ^ bit] = exchange(a, bit, n)
    return [(ups[r], None) for r in range(n)], [(downs[r], None) for r in range(n)], marks


def body(n, tokens, out_grad, up_weight, down_weight, up_index, down_index):
    width = tokens.shape[1]
    blocks = up_weight.shape[0]
    per_chunk, per_group = blocks // CHUNKS, blocks // 2
    me = lax.axis_index("fsdp").astype(jnp.int32).reshape(1)

    both = jnp.concatenate([tokens, out_grad], axis=1)
    mine = lax.all_gather(both, "tensor", axis=0, tiled=True)
    swapped = exchange(both, 1, n)

    def forward_group(g, rows, *partial):
        return forward(
            n, g * per_group, per_group, me, up_index, down_index, rows, ups[g], downs[g], *partial
        )

    up, down, marks = gather(n, up_weight[:per_group], down_weight[:per_group])
    other = lax.all_gather(after(swapped, *marks), "tensor", axis=0, tiled=True)
    ups, downs = [up], [down]
    h, partial = forward_group(0, mine)
    hs = [h]
    ends = (up[-1][0], down[-1][0])
    up, down = after(up_weight[per_group:], *ends), after(down_weight[per_group:], *ends)
    up, down, marks = gather(n, up, down, (h,))
    ups.append(up)
    downs.append(down)

    def grad_chunk(c, *earlier):
        g, at = c * per_chunk // per_group, c * per_chunk % per_group
        rows = after(other, *earlier)
        up, down, *sent = grads(
            n, g * per_group, at, per_chunk, me, up_index, down_index, mine, rows, hs[g], ups[g], downs[g]
        )
        return up, down, sent, [exchange(part, 2 * (e + 1), n) for e, part in enumerate(sent)]

    parts = [grad_chunk(0, *marks)]
    h, total = forward_group(1, after(mine, *parts[0][2]), partial)
    hs.append(h)
    sums = lax.psum_scatter(after(total, *parts[0][3]), "tensor", scatter_dimension=0, tiled=True)
    for c in range(1, CHUNKS):
        parts.append(grad_chunk(c, total, *parts[c - 1][2]))

    grad_out = ()
    for c, (up, down, _, got) in enumerate(parts):
        grad_out = finish(c * per_chunk, blocks, up, down, got, grad_out)
    return (sums[:, :width], sums[:, width:], *grad_out)


def solution(mesh):
    return jax.shard_map(
        functools.partial(body, mesh.shape["fsdp"]),
        mesh=mesh,
        in_specs=(
            P(("fsdp", "tensor"), None),
            P(("fsdp", "tensor"), None),
            P("tensor", "fsdp", None, None),
            P("tensor", "fsdp", None, None),
            P("tensor", None),
            P("tensor", None),
        ),
        out_specs=(
            P(("fsdp", "tensor"), None),
            P(("fsdp", "tensor"), None),
            P("tensor", "fsdp", None, None),
            P("tensor", "fsdp", None, None),
        ),
        check_vma=False,
    )
```

```python
import functools

import jax
import jax.numpy as jnp
from jax import lax
from jax.experimental import pallas as pl
from jax.experimental.pallas import tpu as pltpu
from jax.sharding import PartitionSpec as P

BLK = 128
CHUNKS = 4
MIB = 1 << 20
US = 3.69e6
NT = (((1,), (1,)), ((), ()))
TN = (((0,), (0,)), ((), ()))


def dot(a, b, dims=(((1,), (0,)), ((), ()))):
    return lax.dot_general(a, b, dims, preferred_element_type=jnp.float32)


def columns(ref, blocks, offset=0):
    parts = [ref[:, pl.ds(pl.multiple_of(b * BLK + offset, BLK), BLK)] for b in blocks]
    return parts[0] if len(parts) == 1 else jnp.concatenate(parts, axis=1)


def side_by_side(ref, j, slots):
    parts = [ref[j, s] for s in range(slots)]
    return parts[0] if len(parts) == 1 else jnp.concatenate(parts, axis=1)


def hidden_pair(n, j, jj, me, up_idx, down_idx, rows, ups, downs):
    slots = ups[0].shape[1]
    width = rows.shape[1] // 2
    pre = jnp.zeros((rows.shape[0], BLK), jnp.float32)
    grad = jnp.zeros((rows.shape[0], BLK), jnp.float32)
    for r in range(n):
        k = (me ^ r) * slots
        chosen = columns(rows, [up_idx[j, k + s] for s in range(slots)])
        pre = pre + dot(chosen, ups[r][jj].reshape(slots * BLK, BLK))
        picked = columns(rows, [down_idx[j, k + s] for s in range(slots)], width)
        grad = grad + dot(picked, side_by_side(downs[r], jj, slots), NT)
    sigma = jax.nn.sigmoid(pre)
    hidden = (pre * sigma).astype(jnp.bfloat16)
    return hidden, (grad * sigma * (1.0 + pre * (1.0 - sigma))).astype(jnp.bfloat16)


def add_spread(n, j, jj, me, idx, h, ws, total, offset, which):
    slots = ws[0].shape[1]
    for r in range(n):
        k = (me ^ r) * slots
        if which == 0:
            terms = dot(h, side_by_side(ws[r], jj, slots))
        else:
            terms = dot(h, ws[r][jj].reshape(slots * BLK, BLK), NT)
        for s in range(slots):
            at = pl.ds(pl.multiple_of(idx[j, k + s] * BLK + offset, BLK), BLK)
            total[:, at] += terms[:, s * BLK : (s + 1) * BLK]


def forward_kernel(n, firsts, resumed, me_ref, up_idx, down_idx, rows, *refs):
    groups = len(firsts)
    if resumed:
        partial, refs = refs[0], refs[1:]
    ups = [refs[2 * n * g : 2 * n * g + n] for g in range(groups)]
    downs = [refs[2 * n * g + n : 2 * n * (g + 1)] for g in range(groups)]
    hs, out_ref = refs[2 * n * groups : (2 * n + 1) * groups], refs[(2 * n + 1) * groups]
    total = refs[-2] if resumed else out_ref
    per_step = ups[0][0].shape[0]
    width = rows.shape[1] // 2
    step = pl.program_id(0)
    me = me_ref[0]
    if resumed:
        copy = pltpu.make_async_copy(partial, total, refs[-1])

    @pl.when(step == 0)
    def _():
        if resumed:
            copy.start()
        else:

            @pl.loop(0, total.shape[0] // 16)
            def _(i):
                at = pl.ds(pl.multiple_of(i * 16, 16), 16)
                total[at] = jnp.zeros((16, total.shape[1]), total.dtype)

    blocks = [(g, jj) for g in range(groups) for jj in range(per_step)]
    for g, jj in blocks:
        j = firsts[g] + step * per_step + jj
        hidden, pre_grad = hidden_pair(n, j, jj, me, up_idx, down_idx, rows, ups[g], downs[g])
        hs[g][0, jj] = hidden
        hs[g][1, jj] = pre_grad

    if resumed:

        @pl.when(step == 0)
        def _():
            copy.wait()

    for g, jj in blocks:
        j = firsts[g] + step * per_step + jj
        add_spread(n, j, jj, me, down_idx, hs[g][0, jj], downs[g], total, 0, 0)
        add_spread(n, j, jj, me, up_idx, hs[g][1, jj], ups[g], total, width, 1)

    if resumed:

        @pl.when(step == pl.num_programs(0) - 1)
        def _():
            @pl.loop(0, total.shape[0] // 16)
            def _(i):
                at = pl.ds(pl.multiple_of(i * 16, 16), 16)
                out_ref[at] = total[at].astype(out_ref.dtype)


def grad_kernel(n, first, per_step, half, me_ref, up_idx, down_idx, mine_hbm, other_hbm, h_mine, *refs):
    ups, downs, outs = refs[:n], refs[n : 2 * n], refs[2 * n : -4]
    mine, other, h_other, sems = refs[-4:]
    slots = ups[0].shape[1]
    width = mine.shape[1] // 2
    me = me_ref[0]
    step = pl.program_id(0)
    copies = [
        pltpu.make_async_copy(src.at[:, pl.ds(p * width, width)], dst.at[:, pl.ds(p * width, width)], sems.at[i])
        for i, (src, dst, p) in enumerate(
            ((other_hbm, other, 0), (other_hbm, other, 1), (mine_hbm, mine, 0), (mine_hbm, mine, 1))
        )
    ]

    @pl.when(step == 0)
    def _():
        for copy in copies:
            copy.start()
        copies[0].wait()
        copies[1].wait()

    @pl.when(step == half)
    def _():
        copies[2].wait()
        copies[3].wait()

    @pl.when(step < half)
    def _():
        for jj in range(per_step):
            at = step * per_step + jj
            hidden, pre_grad = hidden_pair(
                n, first + at, jj, me, up_idx, down_idx, other, ups, downs
            )
            h_other[0, at] = hidden
            h_other[1, at] = pre_grad

    @pl.when(step >= half)
    def _():
        for jj in range(per_step):
            at = (step - half) * per_step + jj
            j = first + at
            for e, r in enumerate(range(0, n, 2)):
                k = (me ^ r) * slots
                up_cols = [up_idx[j, k + s] for s in range(slots)]
                down_cols = [down_idx[j, k + s] for s in range(slots)]
                up = dot(columns(mine, up_cols), h_mine[1, jj], TN)
                up = up + dot(columns(other, up_cols), h_other[1, at], TN)
                down = dot(h_mine[0, jj], columns(mine, down_cols, width), TN)
                down = down + dot(h_other[0, at], columns(other, down_cols, width), TN)
                for s in range(slots):
                    up_tile = up[s * BLK : (s + 1) * BLK]
                    down_tile = down[:, s * BLK : (s + 1) * BLK]
                    if e == 0:
                        outs[0][jj, s] = up_tile
                        outs[1][jj, s] = down_tile
                    else:
                        outs[1 + e][0, jj, s] = up_tile.astype(jnp.bfloat16)
                        outs[1 + e][1, jj, s] = down_tile.astype(jnp.bfloat16)


def finish_kernel(count, own_up, own_down, *refs):
    up_ref, down_ref = refs[-2:]
    up, down = own_up[...], own_down[...]
    for got in refs[:count]:
        up = up + got[0].astype(jnp.float32)
        down = down + got[1].astype(jnp.float32)
    up_ref[...] = up
    down_ref[...] = down


def smem():
    return pl.BlockSpec(memory_space=pltpu.SMEM)


def whole(shape):
    return pl.BlockSpec(shape, lambda i: (0,) * len(shape), pipeline_mode=pl.Buffered(1))


def params():
    return pltpu.CompilerParams(vmem_limit_bytes=60 * MIB)


def tiles(piece, per_step, index):
    array, lead = piece
    slots = array.shape[-3]
    if lead is None:
        return pl.BlockSpec((per_step, slots, BLK, BLK), lambda i: (index(i), 0, 0, 0))
    return pl.BlockSpec((None, per_step, slots, BLK, BLK), lambda i: (lead, index(i), 0, 0, 0))


def forward(n, first, per_group, me, up_index, down_index, rows, ups, downs, partial=None):
    resumed = partial is not None
    count = rows.shape[0]
    per_step = min(4, per_group)
    h_spec = pl.BlockSpec((2, per_step, count, BLK), lambda i: (0, i, 0, 0))
    h_shape = jax.ShapeDtypeStruct((2, per_group, count, BLK), jnp.bfloat16)
    total = jax.ShapeDtypeStruct(rows.shape, jnp.bfloat16 if resumed else jnp.float32)
    scratch = [pltpu.VMEM(rows.shape, jnp.float32), pltpu.SemaphoreType.DMA]
    pieces = ups + downs
    return pl.pallas_call(
        functools.partial(forward_kernel, n, [first], resumed),
        grid=(per_group // per_step,),
        in_specs=[smem()] * 3
        + [whole(rows.shape)]
        + [pl.BlockSpec(memory_space=pl.ANY)] * resumed
        + [tiles(piece, per_step, lambda i: i) for piece in pieces],
        out_specs=[h_spec, whole(rows.shape)],
        out_shape=[h_shape, total],
        scratch_shapes=scratch * resumed,
        compiler_params=params(),
        cost_estimate=pl.CostEstimate(flops=0, bytes_accessed=int(20 * US), transcendentals=0),
        name="forward_last" if resumed else "forward_first",
    )(
        me,
        up_index,
        down_index,
        rows,
        *([partial] if resumed else []),
        *[array for array, _ in pieces],
    )


def grads(n, start, at, per_chunk, me, up_index, down_index, mine, other, h_mine, ups, downs):
    slots = ups[0][0].shape[-3]
    count = h_mine.shape[2]
    per_step = min(4, per_chunk)
    skip = at // per_step
    half = per_chunk // per_step

    def early(i):
        return jnp.minimum(i, half - 1)

    def late(i):
        return jnp.maximum(i - half, 0)

    h_spec = pl.BlockSpec((2, per_step, count, BLK), lambda i: (0, skip + late(i), 0, 0))
    pieces = ups + downs
    w_specs = [tiles(piece, per_step, lambda i: skip + early(i)) for piece in pieces]
    own = pl.BlockSpec((per_step, slots, BLK, BLK), lambda i: (late(i), 0, 0, 0))
    sent = pl.BlockSpec((2, per_step, slots, BLK, BLK), lambda i: (0, late(i), 0, 0, 0))
    own_shape = jax.ShapeDtypeStruct((per_chunk, slots, BLK, BLK), jnp.float32)
    sent_shape = jax.ShapeDtypeStruct((2, per_chunk, slots, BLK, BLK), jnp.bfloat16)
    return pl.pallas_call(
        functools.partial(grad_kernel, n, start + at, per_step, half),
        grid=(2 * half,),
        in_specs=[smem()] * 3 + [pl.BlockSpec(memory_space=pl.ANY)] * 2 + [h_spec] + w_specs,
        out_specs=[own] * 2 + [sent] * (n // 2 - 1),
        out_shape=[own_shape] * 2 + [sent_shape] * (n // 2 - 1),
        scratch_shapes=[
            pltpu.VMEM(mine.shape, mine.dtype),
            pltpu.VMEM(mine.shape, mine.dtype),
            pltpu.VMEM((2, per_chunk, count, BLK), jnp.bfloat16),
            pltpu.SemaphoreType.DMA((4,)),
        ],
        compiler_params=params(),
        cost_estimate=pl.CostEstimate(flops=0, bytes_accessed=int(12 * US), transcendentals=0),
        name="grad_chunk",
    )(me, up_index, down_index, mine, other, h_mine, *[array for array, _ in pieces])


def finish(first, blocks, up, down, got, done):
    per_chunk, slots = up.shape[:2]
    per_step = 4
    at = first // per_step
    own = pl.BlockSpec((per_step, slots, BLK, BLK), lambda i: (i, 0, 0, 0))
    sent = pl.BlockSpec((2, per_step, slots, BLK, BLK), lambda i: (0, i, 0, 0, 0))
    part = pl.BlockSpec((per_step, slots, BLK, BLK), lambda i: (at + i, 0, 0, 0))
    kept = pl.BlockSpec(memory_space=pl.ANY)
    shape = jax.ShapeDtypeStruct((blocks, slots, BLK, BLK), jnp.float32)
    return pl.pallas_call(
        functools.partial(finish_kernel, len(got)),
        grid=(per_chunk // per_step,),
        in_specs=[own] * 2 + [sent] * len(got) + [kept] * len(done),
        out_specs=[part] * 2,
        out_shape=[shape] * 2,
        input_output_aliases={2 + len(got) + i: i for i in range(len(done))},
        compiler_params=params(),
        cost_estimate=pl.CostEstimate(flops=0, bytes_accessed=int(3 * US), transcendentals=0),
        name="finish_chunk",
    )(up, down, *got, *done)


def after(a, *earlier):
    return lax.optimization_barrier((a,) + earlier)[0]


def exchange(a, bit, n):
    return lax.ppermute(a, "fsdp", [(i, i ^ bit) for i in range(n)])


def gather(n, up, down, late=()):
    bits = [1 << b for b in range(n.bit_length() - 1)]
    first, last = bits[0], bits[-1]
    ups = {0: up, first: exchange(up, first, n), last: exchange(up, last, n)}
    downs = {0: down, first: exchange(down, first, n), last: exchange(down, last, n)}
    marks = [ups[first], downs[last], ups[last], downs[first]]
    for held, order in ((ups, bits[1:]), (downs, bits[-2::-1])):
        for bit in order:
            for r in list(held):
                if r ^ bit not in held:
                    a = after(held[r], *marks, *late) if late else held[r]
                    held[r ^ bit] = exchange(a, bit, n)
    return [(ups[r], None) for r in range(n)], [(downs[r], None) for r in range(n)], marks


def body(n, tokens, out_grad, up_weight, down_weight, up_index, down_index):
    width = tokens.shape[1]
    blocks = up_weight.shape[0]
    per_chunk, per_group = blocks // CHUNKS, blocks // 2
    me = lax.axis_index("fsdp").astype(jnp.int32).reshape(1)

    both = jnp.concatenate([tokens, out_grad], axis=1)
    mine = lax.all_gather(both, "tensor", axis=0, tiled=True)
    swapped = exchange(both, 1, n)

    def forward_group(g, rows, *partial):
        return forward(
            n, g * per_group, per_group, me, up_index, down_index, rows, ups[g], downs[g], *partial
        )

    up, down, marks = gather(n, up_weight[:per_group], down_weight[:per_group])
    other = lax.all_gather(after(swapped, *marks), "tensor", axis=0, tiled=True)
    ups, downs = [up], [down]
    h, partial = forward_group(0, mine)
    hs = [h]
    ends = (up[-1][0], down[-1][0])
    up, down = after(up_weight[per_group:], *ends), after(down_weight[per_group:], *ends)
    up, down, marks = gather(n, up, down, (h,))
    ups.append(up)
    downs.append(down)

    def grad_chunk(c, *earlier):
        g, at = c * per_chunk // per_group, c * per_chunk % per_group
        rows = after(other, *earlier)
        up, down, *sent = grads(
            n, g * per_group, at, per_chunk, me, up_index, down_index, mine, rows, hs[g], ups[g], downs[g]
        )
        return up, down, sent, [exchange(part, 2 * (e + 1), n) for e, part in enumerate(sent)]

    parts = [grad_chunk(0, *marks)]
    parts.append(grad_chunk(1, *parts[0][2]))
    h, total = forward_group(1, after(mine, *parts[1][2]), partial)
    hs.append(h)
    sums = lax.psum_scatter(after(total, *parts[0][3]), "tensor", scatter_dimension=0, tiled=True)
    for c in range(2, CHUNKS):
        parts.append(grad_chunk(c, total, *parts[c - 1][2]))

    grad_out = ()
    for c, (up, down, _, got) in enumerate(parts):
        up = after(up, *parts[-1][2])
        grad_out = finish(c * per_chunk, blocks, up, down, got, grad_out)
    return (sums[:, :width], sums[:, width:], *grad_out)


def solution(mesh):
    return jax.shard_map(
        functools.partial(body, mesh.shape["fsdp"]),
        mesh=mesh,
        in_specs=(
            P(("fsdp", "tensor"), None),
            P(("fsdp", "tensor"), None),
            P("tensor", "fsdp", None, None),
            P("tensor", "fsdp", None, None),
            P("tensor", None),
            P("tensor", None),
        ),
        out_specs=(
            P(("fsdp", "tensor"), None),
            P(("fsdp", "tensor"), None),
            P("tensor", "fsdp", None, None),
            P("tensor", "fsdp", None, None),
        ),
        check_vma=False,
    )
```

```python
import functools

import jax
import jax.numpy as jnp
from jax import lax
from jax.experimental import pallas as pl
from jax.experimental.pallas import tpu as pltpu
from jax.sharding import PartitionSpec as P

BLK = 128
CHUNKS = 4
MIB = 1 << 20
US = 3.69e6
NT = (((1,), (1,)), ((), ()))
TN = (((0,), (0,)), ((), ()))


def dot(a, b, dims=(((1,), (0,)), ((), ()))):
    return lax.dot_general(a, b, dims, preferred_element_type=jnp.float32)


def columns(ref, blocks, offset=0):
    parts = [ref[:, pl.ds(pl.multiple_of(b * BLK + offset, BLK), BLK)] for b in blocks]
    return parts[0] if len(parts) == 1 else jnp.concatenate(parts, axis=1)


def side_by_side(ref, j, slots):
    parts = [ref[j, s] for s in range(slots)]
    return parts[0] if len(parts) == 1 else jnp.concatenate(parts, axis=1)


def hidden_pair(n, j, jj, me, up_idx, down_idx, rows, ups, downs):
    slots = ups[0].shape[1]
    width = rows.shape[1] // 2
    pre = jnp.zeros((rows.shape[0], BLK), jnp.float32)
    grad = jnp.zeros((rows.shape[0], BLK), jnp.float32)
    for r in range(n):
        k = (me ^ r) * slots
        chosen = columns(rows, [up_idx[j, k + s] for s in range(slots)])
        pre = pre + dot(chosen, ups[r][jj].reshape(slots * BLK, BLK))
        picked = columns(rows, [down_idx[j, k + s] for s in range(slots)], width)
        grad = grad + dot(picked, side_by_side(downs[r], jj, slots), NT)
    sigma = jax.nn.sigmoid(pre)
    hidden = (pre * sigma).astype(jnp.bfloat16)
    return hidden, (grad * sigma * (1.0 + pre * (1.0 - sigma))).astype(jnp.bfloat16)


def add_spread(n, j, jj, me, idx, h, ws, total, offset, which):
    slots = ws[0].shape[1]
    for r in range(n):
        k = (me ^ r) * slots
        if which == 0:
            terms = dot(h, side_by_side(ws[r], jj, slots))
        else:
            terms = dot(h, ws[r][jj].reshape(slots * BLK, BLK), NT)
        for s in range(slots):
            at = pl.ds(pl.multiple_of(idx[j, k + s] * BLK + offset, BLK), BLK)
            total[:, at] += terms[:, s * BLK : (s + 1) * BLK]


def forward_kernel(n, first, half, resumed, me_ref, up_idx, down_idx, rows, *refs):
    if resumed:
        partial, refs = refs[0], refs[1:]
    ups, downs, (h_ref, out_ref) = refs[:n], refs[n : 2 * n], refs[2 * n : 2 * n + 2]
    total, held = refs[-5:-3] if resumed else (out_ref, refs[-1])
    per_step = ups[0].shape[0]
    inner = min(4, per_step)
    width = rows.shape[1] // 2
    step = pl.program_id(0)
    me = me_ref[0]
    if resumed:
        rounded, sem, out_sems = refs[-3:]
        copy = pltpu.make_async_copy(partial, total, sem)

    @pl.when(step == 0)
    def _():
        if resumed:
            copy.start()
        else:

            @pl.loop(0, total.shape[0] // 16)
            def _(i):
                at = pl.ds(pl.multiple_of(i * 16, 16), 16)
                total[at] = jnp.zeros((16, total.shape[1]), total.dtype)

    @pl.when(step < half)
    def _():
        @pl.loop(0, per_step // inner)
        def _(i):
            for jj in [i * inner + p for p in range(inner)]:
                at = step * per_step + jj
                hidden, pre_grad = hidden_pair(
                    n, first + at, jj, me, up_idx, down_idx, rows, ups, downs
                )
                h_ref[0, jj] = hidden
                h_ref[1, jj] = pre_grad
                held[0, at] = hidden
                held[1, at] = pre_grad

    if resumed:

        @pl.when(step == half)
        def _():
            copy.wait()

    @pl.when(step >= half)
    def _():
        @pl.loop(0, per_step // inner)
        def _(i):
            for jj in [i * inner + p for p in range(inner)]:
                at = (step - half) * per_step + jj
                j = first + at
                add_spread(n, j, jj, me, down_idx, held[0, at], downs, total, 0, 0)
                add_spread(n, j, jj, me, up_idx, held[1, at], ups, total, width, 1)

    if resumed:

        @pl.when(step == pl.num_programs(0) - 1)
        def _():
            part = total.shape[0] // 4
            writes = []
            for q in range(4):

                @pl.loop(0, part // 16)
                def _(i, q=q):
                    at = pl.ds(pl.multiple_of(q * part + i * 16, 16), 16)
                    rounded[at] = total[at].astype(rounded.dtype)

                span = pl.ds(q * part, part)
                writes.append(
                    pltpu.make_async_copy(rounded.at[span], out_ref.at[span], out_sems.at[q])
                )
                writes[-1].start()
            for write in writes:
                write.wait()


def grad_kernel(n, first, per_step, half, me_ref, up_idx, down_idx, mine_hbm, other_hbm, h_mine, *refs):
    ups, downs, outs = refs[:n], refs[n : 2 * n], refs[2 * n : -4]
    mine, other, h_other, sems = refs[-4:]
    slots = ups[0].shape[1]
    width = mine.shape[1] // 2
    me = me_ref[0]
    step = pl.program_id(0)
    copies = [
        pltpu.make_async_copy(src.at[:, pl.ds(p * width, width)], dst.at[:, pl.ds(p * width, width)], sems.at[i])
        for i, (src, dst, p) in enumerate(
            ((other_hbm, other, 0), (other_hbm, other, 1), (mine_hbm, mine, 0), (mine_hbm, mine, 1))
        )
    ]

    @pl.when(step == 0)
    def _():
        for copy in copies:
            copy.start()
        copies[0].wait()
        copies[1].wait()

    @pl.when(step == half)
    def _():
        copies[2].wait()
        copies[3].wait()

    @pl.when(step < half)
    def _():
        for jj in range(per_step):
            at = step * per_step + jj
            hidden, pre_grad = hidden_pair(
                n, first + at, jj, me, up_idx, down_idx, other, ups, downs
            )
            h_other[0, at] = hidden
            h_other[1, at] = pre_grad

    @pl.when(step >= half)
    def _():
        for jj in range(per_step):
            at = (step - half) * per_step + jj
            j = first + at
            for e, r in enumerate(range(0, n, 2)):
                k = (me ^ r) * slots
                up_cols = [up_idx[j, k + s] for s in range(slots)]
                down_cols = [down_idx[j, k + s] for s in range(slots)]
                up = dot(columns(mine, up_cols), h_mine[1, jj], TN)
                up = up + dot(columns(other, up_cols), h_other[1, at], TN)
                down = dot(h_mine[0, jj], columns(mine, down_cols, width), TN)
                down = down + dot(h_other[0, at], columns(other, down_cols, width), TN)
                for s in range(slots):
                    up_tile = up[s * BLK : (s + 1) * BLK]
                    down_tile = down[:, s * BLK : (s + 1) * BLK]
                    if e == 0:
                        outs[0][jj, s] = up_tile
                        outs[1][jj, s] = down_tile
                    else:
                        outs[1 + e][0, jj, s] = up_tile.astype(jnp.bfloat16)
                        outs[1 + e][1, jj, s] = down_tile.astype(jnp.bfloat16)


def finish_kernel(count, own_up, own_down, *refs):
    up_ref, down_ref = refs[-2:]
    up, down = own_up[...], own_down[...]
    for got in refs[:count]:
        up = up + got[0].astype(jnp.float32)
        down = down + got[1].astype(jnp.float32)
    up_ref[...] = up
    down_ref[...] = down


def smem():
    return pl.BlockSpec(memory_space=pltpu.SMEM)


def whole(shape):
    return pl.BlockSpec(shape, lambda i: (0,) * len(shape), pipeline_mode=pl.Buffered(1))


def params():
    return pltpu.CompilerParams(vmem_limit_bytes=60 * MIB)


def tiles(piece, per_step, index):
    array, lead = piece
    slots = array.shape[-3]
    if lead is None:
        return pl.BlockSpec((per_step, slots, BLK, BLK), lambda i: (index(i), 0, 0, 0))
    return pl.BlockSpec((None, per_step, slots, BLK, BLK), lambda i: (lead, index(i), 0, 0, 0))


def forward(n, first, per_group, me, up_index, down_index, rows, ups, downs, partial=None):
    resumed = partial is not None
    count = rows.shape[0]
    per_step = min(8, per_group)
    half = per_group // per_step
    h_spec = pl.BlockSpec((2, per_step, count, BLK), lambda i: (0, jnp.minimum(i, half - 1), 0, 0))
    h_shape = jax.ShapeDtypeStruct((2, per_group, count, BLK), jnp.bfloat16)
    total = jax.ShapeDtypeStruct(rows.shape, jnp.bfloat16 if resumed else jnp.float32)
    held = pltpu.VMEM(h_shape.shape, h_shape.dtype)
    scratch = [held]
    if resumed:
        scratch = [
            pltpu.VMEM(rows.shape, jnp.float32),
            held,
            pltpu.VMEM(rows.shape, jnp.bfloat16),
            pltpu.SemaphoreType.DMA,
            pltpu.SemaphoreType.DMA((4,)),
        ]
    pieces = ups + downs
    return pl.pallas_call(
        functools.partial(forward_kernel, n, first, half, resumed),
        grid=(2 * half,),
        in_specs=[smem()] * 3
        + [whole(rows.shape)]
        + [pl.BlockSpec(memory_space=pl.ANY)] * resumed
        + [tiles(piece, per_step, lambda i: lax.rem(i, half)) for piece in pieces],
        out_specs=[h_spec, pl.BlockSpec(memory_space=pl.ANY) if resumed else whole(rows.shape)],
        out_shape=[h_shape, total],
        scratch_shapes=scratch,
        compiler_params=params(),
        cost_estimate=pl.CostEstimate(flops=0, bytes_accessed=int(20 * US), transcendentals=0),
        name="forward_last" if resumed else "forward_first",
    )(
        me,
        up_index,
        down_index,
        rows,
        *([partial] if resumed else []),
        *[array for array, _ in pieces],
    )


def grads(n, start, at, per_chunk, me, up_index, down_index, mine, other, h_mine, ups, downs):
    slots = ups[0][0].shape[-3]
    count = h_mine.shape[2]
    per_step = min(4, per_chunk)
    skip = at // per_step
    half = per_chunk // per_step

    def early(i):
        return jnp.minimum(i, half - 1)

    def late(i):
        return jnp.maximum(i - half, 0)

    h_spec = pl.BlockSpec((2, per_step, count, BLK), lambda i: (0, skip + late(i), 0, 0))
    pieces = ups + downs
    w_specs = [tiles(piece, per_step, lambda i: skip + early(i)) for piece in pieces]
    own = pl.BlockSpec((per_step, slots, BLK, BLK), lambda i: (late(i), 0, 0, 0))
    sent = pl.BlockSpec((2, per_step, slots, BLK, BLK), lambda i: (0, late(i), 0, 0, 0))
    own_shape = jax.ShapeDtypeStruct((per_chunk, slots, BLK, BLK), jnp.float32)
    sent_shape = jax.ShapeDtypeStruct((2, per_chunk, slots, BLK, BLK), jnp.bfloat16)
    return pl.pallas_call(
        functools.partial(grad_kernel, n, start + at, per_step, half),
        grid=(2 * half,),
        in_specs=[smem()] * 3 + [pl.BlockSpec(memory_space=pl.ANY)] * 2 + [h_spec] + w_specs,
        out_specs=[own] * 2 + [sent] * (n // 2 - 1),
        out_shape=[own_shape] * 2 + [sent_shape] * (n // 2 - 1),
        scratch_shapes=[
            pltpu.VMEM(mine.shape, mine.dtype),
            pltpu.VMEM(mine.shape, mine.dtype),
            pltpu.VMEM((2, per_chunk, count, BLK), jnp.bfloat16),
            pltpu.SemaphoreType.DMA((4,)),
        ],
        compiler_params=params(),
        cost_estimate=pl.CostEstimate(flops=0, bytes_accessed=int(12 * US), transcendentals=0),
        name="grad_chunk",
    )(me, up_index, down_index, mine, other, h_mine, *[array for array, _ in pieces])


def finish(first, blocks, up, down, got, done):
    per_chunk, slots = up.shape[:2]
    per_step = 4
    at = first // per_step
    own = pl.BlockSpec((per_step, slots, BLK, BLK), lambda i: (i, 0, 0, 0))
    sent = pl.BlockSpec((2, per_step, slots, BLK, BLK), lambda i: (0, i, 0, 0, 0))
    part = pl.BlockSpec((per_step, slots, BLK, BLK), lambda i: (at + i, 0, 0, 0))
    kept = pl.BlockSpec(memory_space=pl.ANY)
    shape = jax.ShapeDtypeStruct((blocks, slots, BLK, BLK), jnp.float32)
    return pl.pallas_call(
        functools.partial(finish_kernel, len(got)),
        grid=(per_chunk // per_step,),
        in_specs=[own] * 2 + [sent] * len(got) + [kept] * len(done),
        out_specs=[part] * 2,
        out_shape=[shape] * 2,
        input_output_aliases={2 + len(got) + i: i for i in range(len(done))},
        compiler_params=params(),
        cost_estimate=pl.CostEstimate(flops=0, bytes_accessed=int(3 * US), transcendentals=0),
        name="finish_chunk",
    )(up, down, *got, *done)


def after(a, *earlier):
    return lax.optimization_barrier((a,) + earlier)[0]


def exchange(a, bit, n):
    return lax.ppermute(a, "fsdp", [(i, i ^ bit) for i in range(n)])


def gather(n, up, down, late=()):
    bits = [1 << b for b in range(n.bit_length() - 1)]
    first, last = bits[0], bits[-1]
    ups = {0: up, first: exchange(up, first, n), last: exchange(up, last, n)}
    downs = {0: down, first: exchange(down, first, n), last: exchange(down, last, n)}
    marks = [ups[first], downs[last], ups[last], downs[first]]
    for held, order in ((ups, bits[1:]), (downs, bits[-2::-1])):
        for bit in order:
            for r in list(held):
                if r ^ bit not in held:
                    a = after(held[r], *marks, *late) if late else held[r]
                    held[r ^ bit] = exchange(a, bit, n)
    return [(ups[r], None) for r in range(n)], [(downs[r], None) for r in range(n)], marks


def body(n, tokens, out_grad, up_weight, down_weight, up_index, down_index):
    width = tokens.shape[1]
    blocks = up_weight.shape[0]
    per_chunk, per_group = blocks // CHUNKS, blocks // 2
    me = lax.axis_index("fsdp").astype(jnp.int32).reshape(1)

    both = jnp.concatenate([tokens, out_grad], axis=1)
    mine = lax.all_gather(both, "tensor", axis=0, tiled=True)
    swapped = exchange(both, 1, n)

    def forward_group(g, rows, *partial):
        return forward(
            n, g * per_group, per_group, me, up_index, down_index, rows, ups[g], downs[g], *partial
        )

    up, down, marks = gather(n, up_weight[:per_group], down_weight[:per_group])
    other = lax.all_gather(after(swapped, *marks), "tensor", axis=0, tiled=True)
    ups, downs = [up], [down]
    h, partial = forward_group(0, mine)
    hs = [h]
    ends = (up[-1][0], down[-1][0])
    up, down = after(up_weight[per_group:], *ends), after(down_weight[per_group:], *ends)
    up, down, marks = gather(n, up, down, (h,))
    ups.append(up)
    downs.append(down)

    def grad_chunk(c, *earlier):
        g, at = c * per_chunk // per_group, c * per_chunk % per_group
        rows = after(other, *earlier)
        up, down, *sent = grads(
            n, g * per_group, at, per_chunk, me, up_index, down_index, mine, rows, hs[g], ups[g], downs[g]
        )
        return up, down, sent, [exchange(part, 2 * (e + 1), n) for e, part in enumerate(sent)]

    parts = [grad_chunk(0, *marks)]
    parts.append(grad_chunk(1, *parts[0][2]))
    h, total = forward_group(1, after(mine, *parts[1][2]), partial)
    hs.append(h)
    sums = lax.psum_scatter(after(total, *parts[0][3]), "tensor", scatter_dimension=0, tiled=True)
    for c in range(2, CHUNKS):
        parts.append(grad_chunk(c, total, *parts[c - 1][2]))

    grad_out = ()
    for c, (up, down, _, got) in enumerate(parts):
        up = after(up, *parts[-1][2])
        grad_out = finish(c * per_chunk, blocks, up, down, got, grad_out)
    return (sums[:, :width], sums[:, width:], *grad_out)


def solution(mesh):
    return jax.shard_map(
        functools.partial(body, mesh.shape["fsdp"]),
        mesh=mesh,
        in_specs=(
            P(("fsdp", "tensor"), None),
            P(("fsdp", "tensor"), None),
            P("tensor", "fsdp", None, None),
            P("tensor", "fsdp", None, None),
            P("tensor", None),
            P("tensor", None),
        ),
        out_specs=(
            P(("fsdp", "tensor"), None),
            P(("fsdp", "tensor"), None),
            P("tensor", "fsdp", None, None),
            P("tensor", "fsdp", None, None),
        ),
        check_vma=False,
    )
```

```python
import functools

import jax
import jax.numpy as jnp
from jax import lax
from jax.experimental import pallas as pl
from jax.experimental.pallas import tpu as pltpu
from jax.sharding import PartitionSpec as P

BLK = 128
CHUNKS = 4
MIB = 1 << 20
US = 3.69e6
NT = (((1,), (1,)), ((), ()))
TN = (((0,), (0,)), ((), ()))


def dot(a, b, dims=(((1,), (0,)), ((), ()))):
    return lax.dot_general(a, b, dims, preferred_element_type=jnp.float32)


def columns(ref, blocks, offset=0):
    parts = [ref[:, pl.ds(pl.multiple_of(b * BLK + offset, BLK), BLK)] for b in blocks]
    return parts[0] if len(parts) == 1 else jnp.concatenate(parts, axis=1)


def side_by_side(ref, j, slots):
    parts = [ref[j, s] for s in range(slots)]
    return parts[0] if len(parts) == 1 else jnp.concatenate(parts, axis=1)


def hidden_pair(n, j, jj, me, up_idx, down_idx, rows, ups, downs):
    slots = ups[0].shape[1]
    width = rows.shape[1] // 2
    pre = jnp.zeros((rows.shape[0], BLK), jnp.float32)
    grad = jnp.zeros((rows.shape[0], BLK), jnp.float32)
    for r in range(n):
        k = (me ^ r) * slots
        chosen = columns(rows, [up_idx[j, k + s] for s in range(slots)])
        pre = pre + dot(chosen, ups[r][jj].reshape(slots * BLK, BLK))
        picked = columns(rows, [down_idx[j, k + s] for s in range(slots)], width)
        grad = grad + dot(picked, side_by_side(downs[r], jj, slots), NT)
    sigma = jax.nn.sigmoid(pre)
    hidden = (pre * sigma).astype(jnp.bfloat16)
    return hidden, (grad * sigma * (1.0 + pre * (1.0 - sigma))).astype(jnp.bfloat16)


def add_spread(n, j, jj, me, idx, h, ws, total, offset, which):
    slots = ws[0].shape[1]
    for r in range(n):
        k = (me ^ r) * slots
        if which == 0:
            terms = dot(h, side_by_side(ws[r], jj, slots))
        else:
            terms = dot(h, ws[r][jj].reshape(slots * BLK, BLK), NT)
        for s in range(slots):
            at = pl.ds(pl.multiple_of(idx[j, k + s] * BLK + offset, BLK), BLK)
            total[:, at] += terms[:, s * BLK : (s + 1) * BLK]


def forward_kernel(n, first, half, resumed, me_ref, up_idx, down_idx, rows, *refs):
    if resumed:
        partial, refs = refs[0], refs[1:]
    ups, downs, (h_ref, out_ref) = refs[:n], refs[n : 2 * n], refs[2 * n : 2 * n + 2]
    total, held = refs[-5:-3] if resumed else (out_ref, refs[-1])
    per_step = ups[0].shape[0]
    inner = min(4, per_step)
    width = rows.shape[1] // 2
    step = pl.program_id(0)
    me = me_ref[0]
    if resumed:
        rounded, sem, out_sems = refs[-3:]
        copy = pltpu.make_async_copy(partial, total, sem)

    @pl.when(step == 0)
    def _():
        if resumed:
            copy.start()
        else:

            @pl.loop(0, total.shape[0] // 16)
            def _(i):
                at = pl.ds(pl.multiple_of(i * 16, 16), 16)
                total[at] = jnp.zeros((16, total.shape[1]), total.dtype)

    @pl.when(step < half)
    def _():
        @pl.loop(0, per_step // inner)
        def _(i):
            for jj in [i * inner + p for p in range(inner)]:
                at = step * per_step + jj
                hidden, pre_grad = hidden_pair(
                    n, first + at, jj, me, up_idx, down_idx, rows, ups, downs
                )
                h_ref[0, jj] = hidden
                h_ref[1, jj] = pre_grad
                held[0, at] = hidden
                held[1, at] = pre_grad

    if resumed:

        @pl.when(step == half)
        def _():
            copy.wait()

    @pl.when(step >= half)
    def _():
        @pl.loop(0, per_step // inner)
        def _(i):
            for jj in [i * inner + p for p in range(inner)]:
                at = (step - half) * per_step + jj
                j = first + at
                add_spread(n, j, jj, me, down_idx, held[0, at], downs, total, 0, 0)
                add_spread(n, j, jj, me, up_idx, held[1, at], ups, total, width, 1)

    if resumed:

        @pl.when(step == pl.num_programs(0) - 1)
        def _():
            part = total.shape[0] // 4
            writes = []
            for q in range(4):

                @pl.loop(0, part // 16)
                def _(i, q=q):
                    at = pl.ds(pl.multiple_of(q * part + i * 16, 16), 16)
                    rounded[at] = total[at].astype(rounded.dtype)

                span = pl.ds(q * part, part)
                writes.append(
                    pltpu.make_async_copy(rounded.at[span], out_ref.at[span], out_sems.at[q])
                )
                writes[-1].start()
            for write in writes:
                write.wait()


def grad_kernel(n, first, per_step, half, me_ref, up_idx, down_idx, mine_hbm, other_hbm, h_mine, *refs):
    ups, downs, outs = refs[:n], refs[n : 2 * n], refs[2 * n : -4]
    mine, other, h_other, sems = refs[-4:]
    slots = ups[0].shape[1]
    width = mine.shape[1] // 2
    me = me_ref[0]
    step = pl.program_id(0)
    copies = [
        pltpu.make_async_copy(src.at[:, pl.ds(p * width, width)], dst.at[:, pl.ds(p * width, width)], sems.at[i])
        for i, (src, dst, p) in enumerate(
            ((other_hbm, other, 0), (other_hbm, other, 1), (mine_hbm, mine, 0), (mine_hbm, mine, 1))
        )
    ]

    @pl.when(step == 0)
    def _():
        for copy in copies:
            copy.start()
        copies[0].wait()
        copies[1].wait()

    @pl.when(step == half)
    def _():
        copies[2].wait()
        copies[3].wait()

    @pl.when(step < half)
    def _():
        for jj in range(per_step):
            at = step * per_step + jj
            hidden, pre_grad = hidden_pair(
                n, first + at, jj, me, up_idx, down_idx, other, ups, downs
            )
            h_other[0, at] = hidden
            h_other[1, at] = pre_grad

    @pl.when(step >= half)
    def _():
        for jj in range(per_step):
            at = (step - half) * per_step + jj
            j = first + at
            for e, r in enumerate(range(0, n, 2)):
                k = (me ^ r) * slots
                up_cols = [up_idx[j, k + s] for s in range(slots)]
                down_cols = [down_idx[j, k + s] for s in range(slots)]
                up = dot(columns(mine, up_cols), h_mine[1, jj], TN)
                up = up + dot(columns(other, up_cols), h_other[1, at], TN)
                down = dot(h_mine[0, jj], columns(mine, down_cols, width), TN)
                down = down + dot(h_other[0, at], columns(other, down_cols, width), TN)
                for s in range(slots):
                    up_tile = up[s * BLK : (s + 1) * BLK]
                    down_tile = down[:, s * BLK : (s + 1) * BLK]
                    if e == 0:
                        outs[0][jj, s] = up_tile
                        outs[1][jj, s] = down_tile
                    else:
                        outs[1 + e][0, jj, s] = up_tile.astype(jnp.bfloat16)
                        outs[1 + e][1, jj, s] = down_tile.astype(jnp.bfloat16)


def finish_kernel(count, own_up, own_down, *refs):
    up_ref, down_ref = refs[-2:]
    up, down = own_up[...], own_down[...]
    for got in refs[:count]:
        up = up + got[0].astype(jnp.float32)
        down = down + got[1].astype(jnp.float32)
    up_ref[...] = up
    down_ref[...] = down


def smem():
    return pl.BlockSpec(memory_space=pltpu.SMEM)


def whole(shape):
    return pl.BlockSpec(shape, lambda i: (0,) * len(shape), pipeline_mode=pl.Buffered(1))


def params():
    return pltpu.CompilerParams(vmem_limit_bytes=60 * MIB)


def tiles(piece, per_step, index):
    array, lead = piece
    slots = array.shape[-3]
    if lead is None:
        return pl.BlockSpec((per_step, slots, BLK, BLK), lambda i: (index(i), 0, 0, 0))
    return pl.BlockSpec((None, per_step, slots, BLK, BLK), lambda i: (lead, index(i), 0, 0, 0))


def forward(n, first, per_group, me, up_index, down_index, rows, ups, downs, partial=None):
    resumed = partial is not None
    count = rows.shape[0]
    per_step = min(8, per_group)
    half = per_group // per_step
    h_spec = pl.BlockSpec((2, per_step, count, BLK), lambda i: (0, jnp.minimum(i, half - 1), 0, 0))
    h_shape = jax.ShapeDtypeStruct((2, per_group, count, BLK), jnp.bfloat16)
    total = jax.ShapeDtypeStruct(rows.shape, jnp.bfloat16 if resumed else jnp.float32)
    held = pltpu.VMEM(h_shape.shape, h_shape.dtype)
    scratch = [held]
    if resumed:
        scratch = [
            pltpu.VMEM(rows.shape, jnp.float32),
            held,
            pltpu.VMEM(rows.shape, jnp.bfloat16),
            pltpu.SemaphoreType.DMA,
            pltpu.SemaphoreType.DMA((4,)),
        ]
    pieces = ups + downs
    return pl.pallas_call(
        functools.partial(forward_kernel, n, first, half, resumed),
        grid=(2 * half,),
        in_specs=[smem()] * 3
        + [whole(rows.shape)]
        + [pl.BlockSpec(memory_space=pl.ANY)] * resumed
        + [tiles(piece, per_step, lambda i: lax.rem(i, half)) for piece in pieces],
        out_specs=[h_spec, pl.BlockSpec(memory_space=pl.ANY) if resumed else whole(rows.shape)],
        out_shape=[h_shape, total],
        scratch_shapes=scratch,
        compiler_params=params(),
        cost_estimate=pl.CostEstimate(flops=0, bytes_accessed=int(20 * US), transcendentals=0),
        name="forward_last" if resumed else "forward_first",
    )(
        me,
        up_index,
        down_index,
        rows,
        *([partial] if resumed else []),
        *[array for array, _ in pieces],
    )


def grads(n, start, at, per_chunk, me, up_index, down_index, mine, other, h_mine, ups, downs):
    slots = ups[0][0].shape[-3]
    count = h_mine.shape[2]
    per_step = min(4, per_chunk)
    skip = at // per_step
    half = per_chunk // per_step

    def early(i):
        return jnp.minimum(i, half - 1)

    def late(i):
        return jnp.maximum(i - half, 0)

    h_spec = pl.BlockSpec((2, per_step, count, BLK), lambda i: (0, skip + late(i), 0, 0))
    pieces = ups + downs
    w_specs = [tiles(piece, per_step, lambda i: skip + early(i)) for piece in pieces]
    own = pl.BlockSpec((per_step, slots, BLK, BLK), lambda i: (late(i), 0, 0, 0))
    sent = pl.BlockSpec((2, per_step, slots, BLK, BLK), lambda i: (0, late(i), 0, 0, 0))
    own_shape = jax.ShapeDtypeStruct((per_chunk, slots, BLK, BLK), jnp.float32)
    sent_shape = jax.ShapeDtypeStruct((2, per_chunk, slots, BLK, BLK), jnp.bfloat16)
    return pl.pallas_call(
        functools.partial(grad_kernel, n, start + at, per_step, half),
        grid=(2 * half,),
        in_specs=[smem()] * 3 + [pl.BlockSpec(memory_space=pl.ANY)] * 2 + [h_spec] + w_specs,
        out_specs=[own] * 2 + [sent] * (n // 2 - 1),
        out_shape=[own_shape] * 2 + [sent_shape] * (n // 2 - 1),
        scratch_shapes=[
            pltpu.VMEM(mine.shape, mine.dtype),
            pltpu.VMEM(mine.shape, mine.dtype),
            pltpu.VMEM((2, per_chunk, count, BLK), jnp.bfloat16),
            pltpu.SemaphoreType.DMA((4,)),
        ],
        compiler_params=params(),
        cost_estimate=pl.CostEstimate(flops=0, bytes_accessed=int(12 * US), transcendentals=0),
        name="grad_chunk",
    )(me, up_index, down_index, mine, other, h_mine, *[array for array, _ in pieces])


def finish(first, blocks, up, down, got, done):
    per_chunk, slots = up.shape[:2]
    per_step = 4
    at = first // per_step
    own = pl.BlockSpec((per_step, slots, BLK, BLK), lambda i: (i, 0, 0, 0))
    sent = pl.BlockSpec((2, per_step, slots, BLK, BLK), lambda i: (0, i, 0, 0, 0))
    part = pl.BlockSpec((per_step, slots, BLK, BLK), lambda i: (at + i, 0, 0, 0))
    kept = pl.BlockSpec(memory_space=pl.ANY)
    shape = jax.ShapeDtypeStruct((blocks, slots, BLK, BLK), jnp.float32)
    return pl.pallas_call(
        functools.partial(finish_kernel, len(got)),
        grid=(per_chunk // per_step,),
        in_specs=[own] * 2 + [sent] * len(got) + [kept] * len(done),
        out_specs=[part] * 2,
        out_shape=[shape] * 2,
        input_output_aliases={2 + len(got) + i: i for i in range(len(done))},
        compiler_params=params(),
        cost_estimate=pl.CostEstimate(flops=0, bytes_accessed=int(3 * US), transcendentals=0),
        name="finish_chunk",
    )(up, down, *got, *done)


def after(a, *earlier):
    return lax.optimization_barrier((a,) + earlier)[0]


def exchange(a, bit, n):
    return lax.ppermute(a, "fsdp", [(i, i ^ bit) for i in range(n)])


def gather(n, up, down, ends=(), late=()):
    bits = [1 << b for b in range(n.bit_length() - 1)]
    first, last = bits[0], bits[-1]
    then_up, then_down = (after(up, *ends), after(down, *ends)) if ends else (up, down)
    ups = {0: up, first: exchange(up, first, n), last: exchange(then_up, last, n)}
    downs = {0: down, first: exchange(then_down, first, n), last: exchange(down, last, n)}
    marks = [ups[first], downs[last], ups[last], downs[first]]
    for held, order in ((ups, bits[1:]), (downs, bits[-2::-1])):
        for bit in order:
            for r in list(held):
                if r ^ bit not in held:
                    a = after(held[r], *marks, *late) if late else held[r]
                    held[r ^ bit] = exchange(a, bit, n)
    return [(ups[r], None) for r in range(n)], [(downs[r], None) for r in range(n)], marks


def body(n, tokens, out_grad, up_weight, down_weight, up_index, down_index):
    width = tokens.shape[1]
    blocks = up_weight.shape[0]
    per_chunk, per_group = blocks // CHUNKS, blocks // 2
    me = lax.axis_index("fsdp").astype(jnp.int32).reshape(1)

    both = jnp.concatenate([tokens, out_grad], axis=1)
    mine = lax.all_gather(both, "tensor", axis=0, tiled=True)
    swapped = exchange(both, 1, n)

    def forward_group(g, rows, *partial):
        return forward(
            n, g * per_group, per_group, me, up_index, down_index, rows, ups[g], downs[g], *partial
        )

    up, down, marks = gather(n, up_weight[:per_group], down_weight[:per_group])
    other = lax.all_gather(after(swapped, *marks), "tensor", axis=0, tiled=True)
    ups, downs = [up], [down]
    h, partial = forward_group(0, mine)
    hs = [h]
    ends = (up[-1][0], down[-1][0])
    up, down = after(up_weight[per_group:], *marks), after(down_weight[per_group:], *marks)
    up, down, marks = gather(n, up, down, ends, (h,))
    ups.append(up)
    downs.append(down)

    def grad_chunk(c, *earlier):
        g, at = c * per_chunk // per_group, c * per_chunk % per_group
        rows = after(other, *earlier)
        up, down, *sent = grads(
            n, g * per_group, at, per_chunk, me, up_index, down_index, mine, rows, hs[g], ups[g], downs[g]
        )
        return up, down, sent, [exchange(part, 2 * (e + 1), n) for e, part in enumerate(sent)]

    parts = [grad_chunk(0, *marks)]
    parts.append(grad_chunk(1, *parts[0][2]))
    h, total = forward_group(1, after(mine, *parts[1][2]), partial)
    hs.append(h)
    sums = lax.psum_scatter(after(total, *parts[0][3]), "tensor", scatter_dimension=0, tiled=True)
    for c in range(2, CHUNKS):
        parts.append(grad_chunk(c, total, *parts[c - 1][2]))

    grad_out = ()
    for c, (up, down, _, got) in enumerate(parts):
        up = after(up, *parts[-1][2])
        grad_out = finish(c * per_chunk, blocks, up, down, got, grad_out)
    return (sums[:, :width], sums[:, width:], *grad_out)


def solution(mesh):
    return jax.shard_map(
        functools.partial(body, mesh.shape["fsdp"]),
        mesh=mesh,
        in_specs=(
            P(("fsdp", "tensor"), None),
            P(("fsdp", "tensor"), None),
            P("tensor", "fsdp", None, None),
            P("tensor", "fsdp", None, None),
            P("tensor", None),
            P("tensor", None),
        ),
        out_specs=(
            P(("fsdp", "tensor"), None),
            P(("fsdp", "tensor"), None),
            P("tensor", "fsdp", None, None),
            P("tensor", "fsdp", None, None),
        ),
        check_vma=False,
    )
```

```python
import functools

import jax
import jax.numpy as jnp
from jax import lax
from jax.experimental import pallas as pl
from jax.experimental.pallas import tpu as pltpu
from jax.sharding import PartitionSpec as P

BLK = 128
CHUNKS = 4
MIB = 1 << 20
US = 3.69e6
NT = (((1,), (1,)), ((), ()))
TN = (((0,), (0,)), ((), ()))


def dot(a, b, dims=(((1,), (0,)), ((), ()))):
    return lax.dot_general(a, b, dims, preferred_element_type=jnp.float32)


def columns(ref, blocks, offset=0):
    parts = [ref[:, pl.ds(pl.multiple_of(b * BLK + offset, BLK), BLK)] for b in blocks]
    return parts[0] if len(parts) == 1 else jnp.concatenate(parts, axis=1)


def side_by_side(ref, j, slots):
    parts = [ref[j, s] for s in range(slots)]
    return parts[0] if len(parts) == 1 else jnp.concatenate(parts, axis=1)


def hidden_pair(n, j, jj, me, up_idx, down_idx, rows, ups, downs):
    slots = ups[0].shape[1]
    width = rows.shape[1] // 2
    pre = jnp.zeros((rows.shape[0], BLK), jnp.float32)
    grad = jnp.zeros((rows.shape[0], BLK), jnp.float32)
    for r in range(n):
        k = (me ^ r) * slots
        chosen = columns(rows, [up_idx[j, k + s] for s in range(slots)])
        pre = pre + dot(chosen, ups[r][jj].reshape(slots * BLK, BLK))
        picked = columns(rows, [down_idx[j, k + s] for s in range(slots)], width)
        grad = grad + dot(picked, side_by_side(downs[r], jj, slots), NT)
    sigma = jax.nn.sigmoid(pre)
    hidden = (pre * sigma).astype(jnp.bfloat16)
    return hidden, (grad * sigma * (1.0 + pre * (1.0 - sigma))).astype(jnp.bfloat16)


def add_spread(n, j, jj, me, idx, h, ws, total, offset, which):
    slots = ws[0].shape[1]
    for r in range(n):
        k = (me ^ r) * slots
        if which == 0:
            terms = dot(h, side_by_side(ws[r], jj, slots))
        else:
            terms = dot(h, ws[r][jj].reshape(slots * BLK, BLK), NT)
        for s in range(slots):
            at = pl.ds(pl.multiple_of(idx[j, k + s] * BLK + offset, BLK), BLK)
            total[:, at] += terms[:, s * BLK : (s + 1) * BLK]


def forward_kernel(n, first, half, resumed, me_ref, up_idx, down_idx, rows, *refs):
    if resumed:
        partial, refs = refs[0], refs[1:]
    ups, downs, (h_ref, out_ref) = refs[:n], refs[n : 2 * n], refs[2 * n : 2 * n + 2]
    total, held = refs[-5:-3] if resumed else (out_ref, refs[-1])
    per_step = ups[0].shape[0]
    inner = min(4, per_step)
    width = rows.shape[1] // 2
    step = pl.program_id(0)
    me = me_ref[0]
    if resumed:
        rounded, sem, out_sems = refs[-3:]
        copy = pltpu.make_async_copy(partial, total, sem)

    @pl.when(step == 0)
    def _():
        if resumed:
            copy.start()
        else:

            @pl.loop(0, total.shape[0] // 16)
            def _(i):
                at = pl.ds(pl.multiple_of(i * 16, 16), 16)
                total[at] = jnp.zeros((16, total.shape[1]), total.dtype)

    @pl.when(step < half)
    def _():
        @pl.loop(0, per_step // inner)
        def _(i):
            for jj in [i * inner + p for p in range(inner)]:
                at = step * per_step + jj
                hidden, pre_grad = hidden_pair(
                    n, first + at, jj, me, up_idx, down_idx, rows, ups, downs
                )
                h_ref[0, jj] = hidden
                h_ref[1, jj] = pre_grad
                held[0, at] = hidden
                held[1, at] = pre_grad

    if resumed:

        @pl.when(step == half)
        def _():
            copy.wait()

    @pl.when(step >= half)
    def _():
        @pl.loop(0, per_step // inner)
        def _(i):
            for jj in [i * inner + p for p in range(inner)]:
                at = (step - half) * per_step + jj
                j = first + at
                add_spread(n, j, jj, me, down_idx, held[0, at], downs, total, 0, 0)
                add_spread(n, j, jj, me, up_idx, held[1, at], ups, total, width, 1)

    if resumed:

        @pl.when(step == pl.num_programs(0) - 1)
        def _():
            part = total.shape[0] // 4
            writes = []
            for q in range(4):

                @pl.loop(0, part // 16)
                def _(i, q=q):
                    at = pl.ds(pl.multiple_of(q * part + i * 16, 16), 16)
                    rounded[at] = total[at].astype(rounded.dtype)

                span = pl.ds(q * part, part)
                writes.append(
                    pltpu.make_async_copy(rounded.at[span], out_ref.at[span], out_sems.at[q])
                )
                writes[-1].start()
            for write in writes:
                write.wait()


def grad_kernel(n, first, per_step, half, me_ref, up_idx, down_idx, mine_hbm, other_hbm, h_mine, *refs):
    ups, downs, outs = refs[:n], refs[n : 2 * n], refs[2 * n : -4]
    mine, other, h_other, sems = refs[-4:]
    slots = ups[0].shape[1]
    width = mine.shape[1] // 2
    me = me_ref[0]
    step = pl.program_id(0)
    copies = [
        pltpu.make_async_copy(src.at[:, pl.ds(p * width, width)], dst.at[:, pl.ds(p * width, width)], sems.at[i])
        for i, (src, dst, p) in enumerate(
            ((other_hbm, other, 0), (other_hbm, other, 1), (mine_hbm, mine, 0), (mine_hbm, mine, 1))
        )
    ]

    @pl.when(step == 0)
    def _():
        for copy in copies:
            copy.start()
        copies[0].wait()
        copies[1].wait()

    @pl.when(step == half)
    def _():
        copies[2].wait()
        copies[3].wait()

    @pl.when(step < half)
    def _():
        for jj in range(per_step):
            at = step * per_step + jj
            hidden, pre_grad = hidden_pair(
                n, first + at, jj, me, up_idx, down_idx, other, ups, downs
            )
            h_other[0, at] = hidden
            h_other[1, at] = pre_grad

    @pl.when(step >= half)
    def _():
        for jj in range(per_step):
            at = (step - half) * per_step + jj
            j = first + at
            for e, r in enumerate(range(0, n, 2)):
                k = (me ^ r) * slots
                up_cols = [up_idx[j, k + s] for s in range(slots)]
                down_cols = [down_idx[j, k + s] for s in range(slots)]
                up = dot(columns(mine, up_cols), h_mine[1, jj], TN)
                up = up + dot(columns(other, up_cols), h_other[1, at], TN)
                down = dot(h_mine[0, jj], columns(mine, down_cols, width), TN)
                down = down + dot(h_other[0, at], columns(other, down_cols, width), TN)
                for s in range(slots):
                    up_tile = up[s * BLK : (s + 1) * BLK]
                    down_tile = down[:, s * BLK : (s + 1) * BLK]
                    if e == 0:
                        outs[0][jj, s] = up_tile
                        outs[1][jj, s] = down_tile
                    else:
                        outs[1 + e][0, jj, s] = up_tile.astype(jnp.bfloat16)
                        outs[1 + e][1, jj, s] = down_tile.astype(jnp.bfloat16)


def finish_kernel(count, own_up, own_down, *refs):
    up_ref, down_ref = refs[-2:]
    up, down = own_up[...], own_down[...]
    for got in refs[:count]:
        up = up + got[0].astype(jnp.float32)
        down = down + got[1].astype(jnp.float32)
    up_ref[...] = up
    down_ref[...] = down


def smem():
    return pl.BlockSpec(memory_space=pltpu.SMEM)


def whole(shape):
    return pl.BlockSpec(shape, lambda i: (0,) * len(shape), pipeline_mode=pl.Buffered(1))


def params():
    return pltpu.CompilerParams(vmem_limit_bytes=60 * MIB)


def tiles(piece, per_step, index):
    array, lead = piece
    slots = array.shape[-3]
    if lead is None:
        return pl.BlockSpec((per_step, slots, BLK, BLK), lambda i: (index(i), 0, 0, 0))
    return pl.BlockSpec((None, per_step, slots, BLK, BLK), lambda i: (lead, index(i), 0, 0, 0))


def forward(n, first, per_group, me, up_index, down_index, rows, ups, downs, partial=None):
    resumed = partial is not None
    count = rows.shape[0]
    per_step = min(8, per_group)
    half = per_group // per_step
    h_spec = pl.BlockSpec((2, per_step, count, BLK), lambda i: (0, jnp.minimum(i, half - 1), 0, 0))
    h_shape = jax.ShapeDtypeStruct((2, per_group, count, BLK), jnp.bfloat16)
    total = jax.ShapeDtypeStruct(rows.shape, jnp.bfloat16 if resumed else jnp.float32)
    held = pltpu.VMEM(h_shape.shape, h_shape.dtype)
    scratch = [held]
    if resumed:
        scratch = [
            pltpu.VMEM(rows.shape, jnp.float32),
            held,
            pltpu.VMEM(rows.shape, jnp.bfloat16),
            pltpu.SemaphoreType.DMA,
            pltpu.SemaphoreType.DMA((4,)),
        ]
    pieces = ups + downs
    return pl.pallas_call(
        functools.partial(forward_kernel, n, first, half, resumed),
        grid=(2 * half,),
        in_specs=[smem()] * 3
        + [whole(rows.shape)]
        + [pl.BlockSpec(memory_space=pl.ANY)] * resumed
        + [tiles(piece, per_step, lambda i: lax.rem(i, half)) for piece in pieces],
        out_specs=[h_spec, pl.BlockSpec(memory_space=pl.ANY) if resumed else whole(rows.shape)],
        out_shape=[h_shape, total],
        scratch_shapes=scratch,
        compiler_params=params(),
        cost_estimate=pl.CostEstimate(flops=0, bytes_accessed=int(20 * US), transcendentals=0),
        name="forward_last" if resumed else "forward_first",
    )(
        me,
        up_index,
        down_index,
        rows,
        *([partial] if resumed else []),
        *[array for array, _ in pieces],
    )


def grads(n, start, at, per_chunk, me, up_index, down_index, mine, other, h_mine, ups, downs):
    slots = ups[0][0].shape[-3]
    count = h_mine.shape[2]
    per_step = min(4, per_chunk)
    skip = at // per_step
    half = per_chunk // per_step

    def early(i):
        return jnp.minimum(i, half - 1)

    def late(i):
        return jnp.maximum(i - half, 0)

    h_spec = pl.BlockSpec((2, per_step, count, BLK), lambda i: (0, skip + late(i), 0, 0))
    pieces = ups + downs
    w_specs = [tiles(piece, per_step, lambda i: skip + early(i)) for piece in pieces]
    own = pl.BlockSpec((per_step, slots, BLK, BLK), lambda i: (late(i), 0, 0, 0))
    sent = pl.BlockSpec((2, per_step, slots, BLK, BLK), lambda i: (0, late(i), 0, 0, 0))
    own_shape = jax.ShapeDtypeStruct((per_chunk, slots, BLK, BLK), jnp.float32)
    sent_shape = jax.ShapeDtypeStruct((2, per_chunk, slots, BLK, BLK), jnp.bfloat16)
    return pl.pallas_call(
        functools.partial(grad_kernel, n, start + at, per_step, half),
        grid=(2 * half,),
        in_specs=[smem()] * 3 + [pl.BlockSpec(memory_space=pl.ANY)] * 2 + [h_spec] + w_specs,
        out_specs=[own] * 2 + [sent] * (n // 2 - 1),
        out_shape=[own_shape] * 2 + [sent_shape] * (n // 2 - 1),
        scratch_shapes=[
            pltpu.VMEM(mine.shape, mine.dtype),
            pltpu.VMEM(mine.shape, mine.dtype),
            pltpu.VMEM((2, per_chunk, count, BLK), jnp.bfloat16),
            pltpu.SemaphoreType.DMA((4,)),
        ],
        compiler_params=params(),
        cost_estimate=pl.CostEstimate(flops=0, bytes_accessed=int(12 * US), transcendentals=0),
        name="grad_chunk",
    )(me, up_index, down_index, mine, other, h_mine, *[array for array, _ in pieces])


def finish(first, blocks, up, down, got, done):
    per_chunk, slots = up.shape[:2]
    per_step = 4
    at = first // per_step
    own = pl.BlockSpec((per_step, slots, BLK, BLK), lambda i: (i, 0, 0, 0))
    sent = pl.BlockSpec((2, per_step, slots, BLK, BLK), lambda i: (0, i, 0, 0, 0))
    part = pl.BlockSpec((per_step, slots, BLK, BLK), lambda i: (at + i, 0, 0, 0))
    kept = pl.BlockSpec(memory_space=pl.ANY)
    shape = jax.ShapeDtypeStruct((blocks, slots, BLK, BLK), jnp.float32)
    return pl.pallas_call(
        functools.partial(finish_kernel, len(got)),
        grid=(per_chunk // per_step,),
        in_specs=[own] * 2 + [sent] * len(got) + [kept] * len(done),
        out_specs=[part] * 2,
        out_shape=[shape] * 2,
        input_output_aliases={2 + len(got) + i: i for i in range(len(done))},
        compiler_params=params(),
        cost_estimate=pl.CostEstimate(flops=0, bytes_accessed=int(3 * US), transcendentals=0),
        name="finish_chunk",
    )(up, down, *got, *done)


def after(a, *earlier):
    return lax.optimization_barrier((a,) + earlier)[0]


def exchange(a, bit, n):
    return lax.ppermute(a, "fsdp", [(i, i ^ bit) for i in range(n)])


def gather(n, up, down, ends=(), late=()):
    bits = [1 << b for b in range(n.bit_length() - 1)]
    first, last = bits[0], bits[-1]
    then_up, then_down = (after(up, *ends), after(down, *ends)) if ends else (up, down)
    ups = {0: up, first: exchange(up, first, n), last: exchange(then_up, last, n)}
    downs = {0: down, first: exchange(then_down, first, n), last: exchange(down, last, n)}
    marks = [ups[first], downs[last], ups[last], downs[first]]
    for held, order in ((ups, bits[1:]), (downs, bits[-2::-1])):
        for bit in order:
            for r in list(held):
                if r ^ bit not in held:
                    a = after(held[r], *marks, *late) if late else held[r]
                    held[r ^ bit] = exchange(a, bit, n)
    return [(ups[r], None) for r in range(n)], [(downs[r], None) for r in range(n)], marks


def body(n, tokens, out_grad, up_weight, down_weight, up_index, down_index):
    width = tokens.shape[1]
    blocks = up_weight.shape[0]
    per_chunk, per_group = blocks // CHUNKS, blocks // 2
    me = lax.axis_index("fsdp").astype(jnp.int32).reshape(1)

    both = jnp.concatenate([tokens, out_grad], axis=1)
    mine = lax.all_gather(both, "tensor", axis=0, tiled=True)
    swapped = exchange(both, 1, n)

    def forward_group(g, rows, *partial):
        return forward(
            n, g * per_group, per_group, me, up_index, down_index, rows, ups[g], downs[g], *partial
        )

    up, down, marks = gather(n, up_weight[:per_group], down_weight[:per_group])
    other = lax.all_gather(after(swapped, *marks), "tensor", axis=0, tiled=True)
    ups, downs = [up], [down]
    h, partial = forward_group(0, mine)
    hs = [h]
    ends = (up[-1][0], down[-1][0])
    up, down = after(up_weight[per_group:], *marks), after(down_weight[per_group:], *marks)
    up, down, marks = gather(n, up, down, ends, (h,))
    ups.append(up)
    downs.append(down)

    def swap(sent):
        return [exchange(part, 2 * (e + 1), n) for e, part in enumerate(sent)]

    def grad_chunk(c, *earlier):
        g, at = c * per_chunk // per_group, c * per_chunk % per_group
        rows = after(other, *earlier)
        up, down, *sent = grads(
            n, g * per_group, at, per_chunk, me, up_index, down_index, mine, rows, hs[g], ups[g], downs[g]
        )
        return up, down, sent, [] if c == 0 else swap(sent)

    parts = [grad_chunk(0, *marks)]
    parts.append(grad_chunk(1, *parts[0][2]))
    parts[0][3].extend(swap([after(part, *parts[1][2]) for part in parts[0][2]]))
    h, total = forward_group(1, after(mine, *parts[1][2]), partial)
    hs.append(h)
    sums = lax.psum_scatter(after(total, *parts[0][3]), "tensor", scatter_dimension=0, tiled=True)
    for c in range(2, CHUNKS):
        parts.append(grad_chunk(c, total, *parts[c - 1][2]))

    grad_out = ()
    for c, (up, down, _, got) in enumerate(parts):
        up = after(up, *parts[-1][2])
        grad_out = finish(c * per_chunk, blocks, up, down, got, grad_out)
    return (sums[:, :width], sums[:, width:], *grad_out)


def solution(mesh):
    return jax.shard_map(
        functools.partial(body, mesh.shape["fsdp"]),
        mesh=mesh,
        in_specs=(
            P(("fsdp", "tensor"), None),
            P(("fsdp", "tensor"), None),
            P("tensor", "fsdp", None, None),
            P("tensor", "fsdp", None, None),
            P("tensor", None),
            P("tensor", None),
        ),
        out_specs=(
            P(("fsdp", "tensor"), None),
            P(("fsdp", "tensor"), None),
            P("tensor", "fsdp", None, None),
            P("tensor", "fsdp", None, None),
        ),
        check_vma=False,
    )
```
